512 devices in a mesh: ctx: 64 (over z_lo, x, core), dp: 8 (over z_hi, y).
Axes of the slice: x: 4, y: 4, z: 16 (z_hi: 2, z_lo: 8; z = z_hi * 8 + z_lo), core: 2. Of those that a mesh axis runs over, the one named last changes fastest.
Arguments:
- queries: bfloat16 [8, 8192, 2048], P('dp', 'ctx'), may hold values from -28 to 28
- keys: bfloat16 [8, 8192, 2048], P('dp', 'ctx'), may hold values from -28 to 28
- values: bfloat16 [8, 8192, 2048], P('dp', 'ctx'), may hold values from -6 to 6
- saved_output: bfloat16 [8, 8192, 2048], P('dp', 'ctx'), may hold values from -6 to 6
- d_out: bfloat16 [8, 8192, 2048], P('dp', 'ctx'), may hold values from -16 to 16
- w_out: bfloat16 [2048, 2048], P('dp', 'ctx'), may hold values from -0.125 to 0.125
- block_order: int32 [128], replicated, may hold values from 0 to 127, each once
Outputs:
- d_queries: bfloat16 [8, 8192, 2048], P('dp', 'ctx')
- d_keys: bfloat16 [8, 8192, 2048], P('dp', 'ctx')
- d_values: bfloat16 [8, 8192, 2048], P('dp', 'ctx')
- d_wo: float32 [2048, 2048], P('dp', 'ctx')
The draws below stay inside these ranges and needn't reach their ends.
All inputs are finite; a program needn't handle non-finite values.
Results may differ from the reference program's by a relative error of at most 0.0057.
Values may be sent and summed in bfloat16 or wider, within the bound.
A program may use at most 64 MiB of HBM per device.

```python
import math
import jax
import jax.numpy as jnp
from jax import lax

TOK_DEV = 128
HEADS = 16
DH = 128
DW = 2048
HOPS = 2
HD = 2048
SEQ = 8192
N_CTX = 64
N_DP = 8


def draw_queries(key, part):
    key = jax.random.fold_in(key, 1)
    values = jax.random.normal(key, (N_DP, SEQ, HD), jnp.float32)
    return jnp.clip(values, -28.0, 28.0).astype(jnp.bfloat16)


def draw_keys(key, part):
    key = jax.random.fold_in(key, 2)
    values = jax.random.normal(key, (N_DP, SEQ, HD), jnp.float32)
    return jnp.clip(values, -28.0, 28.0).astype(jnp.bfloat16)


def spiked(result, stream_key, source, target, shards_of, factor):
    owner, partner = [(jnp.arange(result.shape[axis_at]) // (result.shape[axis_at] // shards_of)).reshape([-1 if axis == axis_at else 1 for axis in range(result.ndim)]) for axis_at in (source, target)]
    chosen = jax.random.permutation(stream_key, shards_of)[partner]
    strong = (owner == chosen) | (owner == (partner + shards_of // 2) % shards_of)
    return jnp.where(strong, factor * result, result)


def steps_of(rng, extent, pieces, smallest, largest):
    level, own = 1.0, jax.random.fold_in(rng, 6)
    for dim, parts in pieces:
        draws = jnp.exp(jax.random.uniform(jax.random.fold_in(own, dim), (parts,), jnp.float32, smallest / len(pieces), largest / len(pieces)))
        level = level * jnp.repeat(draws, extent[dim] // parts).reshape([-1 if axis == dim else 1 for axis in range(len(extent))])
    return level


def gaussian(own_key, dims, deviation, limit, pieces=(), held_as=jnp.bfloat16):
    drawn = deviation * jax.random.normal(own_key, dims, jnp.float32)
    if pieces:
        drawn = drawn * steps_of(own_key, dims, pieces, -0.22, 0.18)
    return jnp.clip(drawn, -limit, limit).astype(held_as)


def bell_draw_with(key, shape, spread, reach, shards, heavy, held_as=jnp.bfloat16):
    values = spread * jax.random.normal(key, shape, jnp.float32)
    if shards:
        values = values * steps_of(key, shape, shards, -0.22, 0.18)
    return jnp.clip(spiked(values, jax.random.fold_in(key, 3), *heavy), -reach, reach).astype(held_as)


def setup_inputs(seed: int = 0) -> dict:
    streams_of = jax.random.split(jax.random.key(seed), 8)
    queries = draw_queries(jax.random.fold_in(streams_of[7], 71), 0)
    keys = draw_keys(jax.random.fold_in(streams_of[7], 71), 0)
    values = gaussian(streams_of[2], (N_DP, SEQ, HD), 1.0, 6.0, ((0, 8), (1, 64)))
    saved_output = gaussian(streams_of[3], (N_DP, SEQ, HD), 1.0, 6.0, ((0, 8), (1, 64)))
    d_out = bell_draw_with(streams_of[4], (N_DP, SEQ, DW), 1.0, 16.0, ((0, 8), (1, 64)), (1, 2, 64, 4.0))
    w_out = gaussian(streams_of[5], (HD, DW), HD ** -0.5, 0.125, ((0, 8), (1, 64)))
    block_order = jax.random.permutation(streams_of[6], 2 * N_CTX).astype(jnp.int32)
    return dict(queries=queries, keys=keys, values=values, saved_output=saved_output, d_out=d_out, w_out=w_out, block_order=block_order)


def rounded(values):
    low = lax.optimization_barrier(values.astype(jnp.bfloat16))
    return low.astype(jnp.float32)

def group_places(block_order, groups, tok):
    pairs = block_order.reshape(groups, 2).astype(jnp.int32)
    row_ids = jnp.arange(tok, dtype=jnp.int32)
    half_block = tok // 2
    first = jnp.where(row_ids[None, :] < half_block, pairs[:, 0:1], pairs[:, 1:2])
    return (first * half_block + row_ids[None, :] % half_block).astype(jnp.int32)

def widen(values):
    return jnp.concatenate([jnp.roll(values, distance, axis=0) for distance in range(HOPS + 1)], axis=1)

def narrow(values, tok):
    total = values[:, :tok]
    for distance in range(1, HOPS + 1):
        total = total + jnp.roll(values[:, distance * tok:(distance + 1) * tok], -distance, axis=0)
    return total

def one_sequence(items, places):
    queries, keys, values, saved, d_attn = items
    groups = places.shape[0]
    tok = places.shape[1]
    score_scale = 1.0 / math.sqrt(DH)

    def split(array):
        return array.reshape(groups, tok, HEADS, DH).astype(jnp.float32)
    query_f = split(queries)
    key_wide = widen(split(keys))
    value_wide = widen(split(values))
    saved_f = split(saved)
    grad_f = split(d_attn)
    key_places = widen(places)
    allowed = key_places[:, None, :] <= places[:, :, None]
    scores = jnp.einsum('gqhd,gkhd->ghqk', query_f, key_wide) * score_scale
    masked = jnp.where(allowed[:, None, :, :], scores, -1e+30)
    row_max = lax.optimization_barrier(jnp.max(masked, axis=-1))
    lse = row_max + jnp.log(lax.optimization_barrier(jnp.sum(jnp.exp(masked - row_max[..., None]), axis=-1)))
    probs = jnp.exp(masked - lse[..., None])
    probs_low = rounded(probs)
    delta = jnp.transpose(lax.optimization_barrier(jnp.sum(grad_f * saved_f, axis=-1)), (0, 2, 1))
    d_probs = jnp.einsum('gqhd,gkhd->ghqk', grad_f, value_wide)
    d_scores = rounded(probs * (d_probs - delta[..., None]))
    d_query = jnp.einsum('ghqk,gkhd->gqhd', d_scores, key_wide) * score_scale
    d_key_wide = jnp.einsum('ghqk,gqhd->gkhd', d_scores, query_f) * score_scale
    d_value_wide = jnp.einsum('ghqk,gqhd->gkhd', probs_low, grad_f)
    d_key = narrow(d_key_wide, tok)
    d_value = narrow(d_value_wide, tok)
    shape = (groups * tok, HEADS * DH)
    return (d_query.reshape(shape).astype(jnp.bfloat16), d_key.reshape(shape).astype(jnp.bfloat16), d_value.reshape(shape).astype(jnp.bfloat16))

def reference(queries, keys, values, saved_output, d_out, w_out, block_order):
    places = group_places(block_order, N_CTX, TOK_DEV)
    flat_grad = d_out.reshape(-1, DW)
    d_attn = jnp.dot(flat_grad, w_out.T, preferred_element_type=jnp.float32).astype(jnp.bfloat16)
    d_attn = d_attn.reshape(N_DP, SEQ, HD)
    d_queries, d_keys, d_values = lax.map(lambda items: one_sequence(items, places), (queries, keys, values, saved_output, d_attn))
    grad_scale = 1.0 / math.sqrt(N_DP * SEQ)
    d_wo = jnp.dot(saved_output.reshape(-1, HD).T, flat_grad, preferred_element_type=jnp.float32) * grad_scale
    return (d_queries, d_keys, d_values, d_wo)
```

```python
import math

import jax
import jax.numpy as jnp
from jax import lax
from jax.experimental import pallas as pl
from jax.experimental.pallas import tpu as pltpu
from jax.sharding import PartitionSpec as P

DH = 128
TOK = 128
HEADS = 16
FEAT = 2048
NX, NY, NZ, NZL = 4, 4, 16, 8
SLOTS = 2 * NY
MESH = pl.DeviceIdType.MESH
BF = jnp.bfloat16
F32 = jnp.float32

NT = (((1,), (1,)), ((), ()))
NN = (((1,), (0,)), ((), ()))
TN = (((0,), (0,)), ((), ()))


def dot(a, b, dims):
    return lax.dot_general(a, b, dims, preferred_element_type=F32)


def kernel(
    order_ref, q_in, k_in, v_in, saved_in, grad_in, wt_in,
    dq_ref, dk_ref, dv_ref, dw_ref,
    qb, kb, vb, sv, gb, dab, lse, delta,
    wt, sb, st, dsend, probs, probs_k, ds_own, bias,
    rs_out, rs_in, xs, xr,
    load_s, wx_s, wx_r, zw_s, zw_r, g_s, g_r, sa_s, sa_r, kv_s, kv_r, q_s, q_r,
    da_s, da_r, fw_s, fw_r, fo_s, fo_r, row_s, row_r, zr_s, zr_r, xr_s, xr_r,
):
    ctx = lax.axis_index("ctx")
    dp = lax.axis_index("dp")
    core = lax.rem(ctx, 2)
    x = lax.rem(lax.div(ctx, 2), NX)
    zl = lax.div(ctx, 2 * NX)
    y = lax.rem(dp, NY)
    z = lax.div(dp, NY) * NZL + zl
    n_ctx = 2 * NX * NZL
    me = 2 * y + core

    def at(xx, yy, zz, cc):
        return {
            "ctx": lax.rem(zz, NZL) * (2 * NX) + xx * 2 + cc,
            "dp": lax.div(zz, NZL) * NY + yy,
        }

    other = at(x, y, z, 1 - core)
    after = {"ctx": lax.rem(ctx + 2, n_ctx), "dp": dp}
    before = {"ctx": lax.rem(ctx + n_ctx - 2, n_ctx), "dp": dp}
    yp, ym, yf = lax.rem(y + 1, NY), lax.rem(y + 3, NY), lax.rem(y + 2, NY)
    y_up, y_down = at(x, yp, z, core), at(x, ym, z, core)
    z_up, z_down = at(x, y, lax.rem(z + 1, NZ), core), at(x, y, lax.rem(z + NZ - 1, NZ), core)
    y_group = [(dy, dc) for dy in (1, 3, 2, 0) for dc in (0, 1) if (dy, dc) != (0, 0)]
    x_group = [(dx, dc) for dx in (1, 3, 2, 0) for dc in (0, 1) if (dx, dc) != (0, 0)]

    def y_peer(dy, dc):
        yy, cc = lax.rem(y + dy, NY), lax.rem(core + dc, 2)
        return at(x, yy, z, cc), 2 * yy + cc

    def x_peer(dx, dc):
        xx, cc = lax.rem(x + dx, NX), lax.rem(core + dc, 2)
        return at(xx, y, z, cc), xx, cc

    def send(src, dst, ssem, rsem, device):
        copy = pltpu.make_async_remote_copy(
            src_ref=src, dst_ref=dst, send_sem=ssem, recv_sem=rsem, device_id=device, device_id_type=MESH
        )
        copy.start()

    def took(ref, sem):
        pltpu.make_async_copy(ref, ref, sem).wait()

    own = pl.ds(0, TOK)
    my_rows = pl.ds(pl.multiple_of(me * TOK, TOK), TOK)
    loads = [
        pltpu.make_async_copy(grad_in, gb.at[my_rows, :], load_s.at[0]),
        pltpu.make_async_copy(saved_in, sv, load_s.at[1]),
        pltpu.make_async_copy(k_in, kb.at[own, :], load_s.at[2]),
        pltpu.make_async_copy(q_in, qb.at[own, :], load_s.at[3]),
        pltpu.make_async_copy(v_in, vb.at[own, :], load_s.at[4]),
    ]
    for load in loads:
        load.start()

    barrier = pltpu.get_barrier_semaphore()
    peers = [y_peer(*d)[0] for d in y_group] + [x_peer(*d)[0] for d in x_group if d != (0, 1)]
    peers += [z_up, z_down, after, before]
    for peer in peers:
        pl.semaphore_signal(barrier, inc=1, device_id=peer, device_id_type=MESH)
    pl.semaphore_wait(barrier, len(peers))

    z_lanes = pl.ds(pl.multiple_of(lax.div(z, NZL) * DH, DH), DH)
    piece = pl.ds(pl.multiple_of(ctx * 32, 32), 32)
    for d in x_group:
        dev, xx, cc = x_peer(*d)
        send(wt_in.at[:, pl.ds(pl.multiple_of(cc * DH, DH), DH)], wt.at[piece, z_lanes], wx_s, wx_r, dev)
    wt[piece, z_lanes] = wt_in[:, pl.ds(pl.multiple_of(core * DH, DH), DH)]

    def half(slot, part):
        return gb.at[pl.ds(pl.multiple_of(slot * TOK + part * 64, 64), 64), :]

    def whole(slot):
        return gb.at[pl.ds(pl.multiple_of(slot * TOK, TOK), TOK), :]

    s_up, s_down, s_far = 2 * yp + core, 2 * ym + core, 2 * yf + core
    loads[0].wait()
    send(half(me, 0), half(me, 0), g_s.at[0], g_r.at[0], y_up)
    send(half(me, 1), half(me, 1), g_s.at[1], g_r.at[1], y_down)
    send(half(me, 1), half(me, 1), g_s.at[2], g_r.at[2], y_up)
    send(half(me, 0), half(me, 0), g_s.at[3], g_r.at[3], y_down)
    send(whole(me), whole(me), g_s.at[6], g_r.at[6], other)

    prev2, prev1 = pl.ds(2 * TOK, TOK), pl.ds(TOK, TOK)
    loads[2].wait()
    send(kb.at[own, :], kb.at[prev2, :], kv_s.at[0], kv_r.at[0], after)
    loads[3].wait()
    send(qb.at[own, :], qb.at[prev2, :], q_s.at[0], q_r.at[0], before)
    loads[4].wait()
    send(vb.at[own, :], vb.at[prev2, :], kv_s.at[1], kv_r.at[1], after)

    @pl.when(core == 0)
    def _():
        send(kb.at[own, :], kb.at[prev1, :], kv_s.at[2], kv_r.at[2], other)
        send(vb.at[own, :], vb.at[prev1, :], kv_s.at[3], kv_r.at[3], other)

    @pl.when(core == 1)
    def _():
        send(qb.at[own, :], qb.at[prev1, :], q_s.at[1], q_r.at[1], other)

    loads[1].wait()

    def head_lanes(h):
        return pl.ds(pl.multiple_of(h * DH, DH), DH)

    for d in y_group:
        dev, slot = y_peer(*d)
        for zh in range(2):
            send(sv.at[:, head_lanes(8 * zh + slot)], sb.at[my_rows, pl.ds(zh * DH, DH)], sa_s, sa_r, dev)
    for zh in range(2):
        sb[my_rows, pl.ds(zh * DH, DH)] = sv[:, head_lanes(8 * zh + me)]

    group = ctx
    lane = lax.broadcasted_iota(jnp.int32, (TOK, TOK), 1)
    row = lax.broadcasted_iota(jnp.int32, (TOK, TOK), 0)

    def places(g, index):
        first, second = order_ref[2 * g], order_ref[2 * g + 1]
        return jnp.where(index < 64, first * 64 + index, second * 64 + index - 64)

    def blocked(key_group, query_group):
        seen = places(key_group, row) <= places(query_group, lane)
        return jnp.where(seen, 0.0, -1e30).astype(F32)

    def shifted(by):
        return lax.rem(group + n_ctx + by, n_ctx)

    bias[0] = blocked(group, group)
    bias[1] = blocked(shifted(-1), group)
    bias[2] = blocked(shifted(-2), group)
    bias[3] = blocked(group, shifted(1))
    bias[4] = blocked(group, shifted(2))
    scale = 1.0 / math.sqrt(DH)

    def z_rows(zz, first=0, count=256):
        start = lax.rem(zz, NZL) * 256 + first
        return wt.at[
            pl.ds(pl.multiple_of(start, 128), count),
            pl.ds(pl.multiple_of(lax.div(zz, NZL) * DH, DH), DH),
        ]

    def ring_step(t):
        up = lax.rem(z + NZ - (t - 1), NZ)
        down = lax.rem(z + (t - 1), NZ)
        parts = (0, 256, 0, 256) if t < 8 else (0, 128, 128, 128)
        send(z_rows(up, *parts[:2]), z_rows(up, *parts[:2]), zw_s.at[0, t - 1], zw_r.at[0, t - 1], z_up)
        send(z_rows(down, *parts[2:]), z_rows(down, *parts[2:]), zw_s.at[1, t - 1], zw_r.at[1, t - 1], z_down)

    def ring_wait(sems, t):
        count = 256 if t < 8 else 128
        for way in range(2):
            took(wt.at[pl.ds(0, count), pl.ds(0, DH)], sems.at[way, t - 1])

    took(wt.at[pl.ds(0, 224), pl.ds(0, DH)], wx_r)
    for t in range(1, 9):
        ring_step(t)
        if t == 3:
            took(half(s_down, 0), g_r.at[0])
            send(half(s_down, 0), half(s_down, 0), g_s.at[4], g_r.at[4], y_up)
            took(half(s_up, 1), g_r.at[1])
            send(half(s_up, 1), half(s_up, 1), g_s.at[5], g_r.at[5], y_down)
        if t == 5:
            took(half(s_down, 1), g_r.at[2])
            send(whole(s_down), whole(s_down), g_s.at[7], g_r.at[7], other)
            took(half(s_up, 0), g_r.at[3])
            send(whole(s_up), whole(s_up), g_s.at[8], g_r.at[8], other)
        if t == 6:
            took(kb.at[prev2, :], kv_r.at[0])
            took(qb.at[prev2, :], q_r.at[0])

            @pl.when(core == 1)
            def _():
                send(kb.at[prev2, :], kb.at[prev1, :], kv_s.at[2], kv_r.at[2], other)

            @pl.when(core == 0)
            def _():
                send(qb.at[prev2, :], qb.at[prev1, :], q_s.at[1], q_r.at[1], other)
        ring_wait(zw_r, t)

    took(half(s_far, 0), g_r.at[4])
    took(half(s_far, 1), g_r.at[5])
    send(whole(s_far), whole(s_far), g_s.at[9], g_r.at[9], other)
    for i in range(6, 10):
        took(whole(me), g_r.at[i])

    for dy in (2, 1, 3, 0):
        yy = lax.rem(y + dy, NY)
        rows = pl.ds(pl.multiple_of(yy * 256, 256), 256)
        part = dot(gb[rows, :], wt[...], NN).astype(BF)
        for cc in range(2):
            slot = 2 * yy + cc
            for zh in range(2):
                dsend[slot, zh] = part[cc * TOK : (cc + 1) * TOK, zh * DH : (zh + 1) * DH]
            mine = dab.at[pl.ds(2 * me, 2), own, :]
            if dy != 0:
                send(dsend.at[slot], mine, da_s.at[2 * dy + cc], da_r.at[me], at(x, yy, z, cc))
        if dy == 0:
            send(dsend.at[2 * y + 1 - core], dab.at[pl.ds(2 * me, 2), own, :], da_s.at[0], da_r.at[me], other)
            for zh in range(2):
                dab[2 * me + zh, 0:TOK, :] = dsend[me, zh]

    took(kb.at[prev1, :], kv_r.at[2])

    def score_head(i, carry):
        h = 8 * lax.rem(i, 2) + lax.div(i, 2)
        lanes = head_lanes(h)
        s = dot(kb[:, lanes], qb[own, lanes], NT) * scale
        s = s + bias[0:3].reshape(3 * TOK, TOK)
        top = jnp.max(s, axis=0, keepdims=True)
        e = jnp.exp(s - top)
        total = jnp.sum(e, axis=0, keepdims=True)
        probs[i] = e * (1.0 / total)
        lse[0, i] = top + jnp.log(total)
        return carry

    lax.fori_loop(0, HEADS, score_head, 0)

    near, far = pl.ds(TOK, TOK), pl.ds(2 * TOK, TOK)
    send(lse.at[0], lse.at[2], row_s.at[0], row_r.at[0], before)

    @pl.when(core == 1)
    def _():
        send(lse.at[0], lse.at[1], row_s.at[1], row_r.at[1], other)

    took(vb.at[prev2, :], kv_r.at[1])

    @pl.when(core == 1)
    def _():
        send(vb.at[prev2, :], vb.at[prev1, :], kv_s.at[3], kv_r.at[3], other)

    took(sb.at[pl.ds(0, 896), :], sa_r)
    st[...] = sb[...].astype(F32).T.astype(BF)

    def partial_of(zz):
        zh, low = lax.div(zz, NZL), lax.rem(zz, NZL)
        return dot(
            st[pl.ds(pl.multiple_of(zh * DH, DH), DH), :],
            gb[:, pl.ds(pl.multiple_of(low * 256, 256), 256)],
            NN,
        )

    def sum_step(t):
        up = partial_of(lax.rem(z + 9 - t, NZ))
        if t > 1:
            took(rs_in.at[0, t - 2], zr_r.at[0, t - 2])
            up = up + rs_in[0, t - 2].astype(F32)
        rs_out[0, t - 1] = up.astype(BF)
        send(rs_out.at[0, t - 1], rs_in.at[0, t - 1], zr_s.at[0, t - 1], zr_r.at[0, t - 1], z_up)
        if t < 8:
            down = partial_of(lax.rem(z + NZ - 8 + t, NZ))
            if t > 1:
                took(rs_in.at[1, t - 2], zr_r.at[1, t - 2])
                down = down + rs_in[1, t - 2].astype(F32)
            rs_out[1, t - 1] = down.astype(BF)
            send(rs_out.at[1, t - 1], rs_in.at[1, t - 1], zr_s.at[1, t - 1], zr_r.at[1, t - 1], z_down)

    def chunk(slot, rows):
        return dab.at[pl.ds(2 * slot, 2), rows, :]

    def pass_on(dy, cc):
        slot = 2 * lax.rem(y + dy, NY) + cc
        if dy == 0:
            @pl.when(cc != core)
            def _():
                took(chunk(slot, own), da_r.at[slot])
        else:
            took(chunk(slot, own), da_r.at[slot])
        send(chunk(slot, own), chunk(slot, far), fw_s.at[slot], fw_r.at[slot], before)

        @pl.when(core == 1)
        def _():
            send(chunk(slot, own), chunk(slot, near), fo_s.at[slot], fo_r.at[slot], other)

    sum_step(1)
    for dy in (0, 1, 3):
        for cc in range(2):
            pass_on(dy, cc)
    sum_step(2)
    for cc in range(2):
        pass_on(2, cc)

    ones = jnp.ones((8, DH), BF)

    def delta_head(i, carry):
        h = 8 * lax.rem(i, 2) + lax.div(i, 2)
        prod = dab[i, 0:TOK, :].astype(F32) * sv[:, head_lanes(h)].astype(F32)
        high = prod.astype(BF)
        low = (prod - high.astype(F32)).astype(BF)
        sums = dot(ones, high, NT) + dot(ones, low, NT)
        delta[0, i] = sums[0:1]
        return carry

    lax.fori_loop(0, HEADS, delta_head, 0)
    send(delta.at[0], delta.at[2], row_s.at[2], row_r.at[2], before)

    @pl.when(core == 1)
    def _():
        send(delta.at[0], delta.at[1], row_s.at[3], row_r.at[3], other)

    sum_step(3)

    took(qb.at[near, :], q_r.at[1])
    took(lse.at[2], row_r.at[0])

    @pl.when(core == 0)
    def _():
        send(lse.at[2], lse.at[1], row_s.at[1], row_r.at[1], other)

    took(lse.at[1], row_r.at[1])

    def later_head(i, carry):
        h = 8 * lax.rem(i, 2) + lax.div(i, 2)
        lanes = head_lanes(h)
        s = dot(kb[own, lanes], qb[TOK:, lanes], NT) * scale
        s = s + jnp.concatenate([bias[3], bias[4]], axis=1)
        probs_k[i] = jnp.exp(s - jnp.concatenate([lse[1, i], lse[2, i]], axis=1))
        return carry

    lax.fori_loop(0, HEADS, later_head, 0)
    sum_step(4)

    took(vb.at[prev1, :], kv_r.at[3])

    def own_head(i, carry):
        h = 8 * lax.rem(i, 2) + lax.div(i, 2)
        lanes = head_lanes(h)
        dprobs = dot(vb[:, lanes], dab[i, 0:TOK, :], NT)
        ds = (probs[i] * (dprobs - delta[0, i])).astype(BF)
        ds_own[i] = ds[0:TOK]
        dq_ref[:, lanes] = (dot(ds, kb[:, lanes], TN) * scale).astype(BF)
        return carry

    lax.fori_loop(0, HEADS // 2, own_head, 0)
    sum_step(5)
    lax.fori_loop(HEADS // 2, HEADS, own_head, 0)
    sum_step(6)

    for dy in (0, 1, 3, 2):
        for cc in range(2):
            slot = 2 * lax.rem(y + dy, NY) + cc
            took(chunk(slot, far), fw_r.at[slot])

            @pl.when(core == 0)
            def _():
                send(chunk(slot, far), chunk(slot, near), fo_s.at[slot], fo_r.at[slot], other)
    took(delta.at[2], row_r.at[2])

    @pl.when(core == 0)
    def _():
        send(delta.at[2], delta.at[1], row_s.at[3], row_r.at[3], other)

    sum_step(7)
    for slot in range(SLOTS):
        took(chunk(slot, near), fo_r.at[slot])
    took(delta.at[1], row_r.at[3])
    sum_step(8)

    def key_head(i, carry):
        h = 8 * lax.rem(i, 2) + lax.div(i, 2)
        lanes = head_lanes(h)
        later = dab[i, TOK:, :]
        p = probs_k[i]
        dprobs = dot(vb[own, lanes], later, NT)
        ds = (p * (dprobs - jnp.concatenate([delta[1, i], delta[2, i]], axis=1))).astype(BF)
        dkey = dot(ds_own[i], qb[own, lanes], NN) + dot(ds, qb[TOK:, lanes], NN)
        dk_ref[:, lanes] = (dkey * scale).astype(BF)
        dval = dot(probs[i, 0:TOK, :].astype(BF), dab[i, 0:TOK, :], NN) + dot(p.astype(BF), later, NN)
        dv_ref[:, lanes] = dval.astype(BF)
        return carry

    lax.fori_loop(0, HEADS, key_head, 0)

    total = partial_of(z)
    took(rs_in.at[0, 7], zr_r.at[0, 7])
    total = total + rs_in[0, 7].astype(F32)
    took(rs_in.at[1, 6], zr_r.at[1, 6])
    total = total + rs_in[1, 6].astype(F32)
    xs[...] = total.T
    for d in x_group:
        dev, xx, cc = x_peer(*d)
        rows = pl.ds(pl.multiple_of((2 * xx + cc) * 32, 32), 32)
        send(xs.at[rows, :], xr.at[2 * x + core], xr_s, xr_r, dev)
    xr[2 * x + core] = xs[pl.ds(pl.multiple_of((2 * x + core) * 32, 32), 32), :]
    took(xr.at[pl.ds(0, 7)], xr_r)
    grad_scale = 1.0 / math.sqrt(8 * n_ctx * TOK)
    for cc in range(2):
        both = (xr[cc] + xr[2 + cc]) + (xr[4 + cc] + xr[6 + cc])
        dw_ref[cc * DH : (cc + 1) * DH, :] = (both * grad_scale).T

    took(wt.at[pl.ds(0, 224), pl.ds(0, DH)], wx_s)
    for t in range(1, 9):
        ring_wait(zw_s, t)
        took(rs_out.at[0, t - 1], zr_s.at[0, t - 1])
        if t < 8:
            took(rs_out.at[1, t - 1], zr_s.at[1, t - 1])
    for i in range(6):
        took(half(me, 0), g_s.at[i])
    for i in range(6, 10):
        took(whole(me), g_s.at[i])
    took(sb.at[pl.ds(0, 896), :], sa_s)
    for i in range(4):
        took(kb.at[own, :], kv_s.at[i])
        took(lse.at[0], row_s.at[i])
    for i in range(2):
        took(qb.at[own, :], q_s.at[i])
    for i in [0, 2, 3, 4, 5, 6, 7]:
        took(dsend.at[0], da_s.at[i])
    for slot in range(SLOTS):
        took(chunk(slot, own), fw_s.at[slot])
        took(chunk(slot, own), fo_s.at[slot])
    took(xr.at[pl.ds(0, 7)], xr_s)


def per_device(queries, keys, values, saved_output, d_out, w_out, block_order):
    sems = pltpu.SemaphoreType.DMA
    vmem = pltpu.VMEM
    tokens = jax.ShapeDtypeStruct((TOK, FEAT), BF)
    anywhere = pl.BlockSpec(memory_space=pl.ANY)
    inside = pl.BlockSpec(memory_space=pltpu.VMEM)
    dq, dk, dv, dw = pl.pallas_call(
        kernel,
        out_shape=(tokens, tokens, tokens, jax.ShapeDtypeStruct((256, 32), F32)),
        in_specs=[pl.BlockSpec(memory_space=pltpu.SMEM)] + [anywhere] * 5 + [inside],
        out_specs=(inside,) * 4,
        scratch_shapes=[
            vmem((3 * TOK, FEAT), BF),
            vmem((3 * TOK, FEAT), BF),
            vmem((3 * TOK, FEAT), BF),
            vmem((TOK, FEAT), BF),
            vmem((SLOTS * TOK, FEAT), BF),
            vmem((HEADS, 3 * TOK, DH), BF),
            vmem((3, HEADS, 1, TOK), F32),
            vmem((3, HEADS, 1, TOK), F32),
            vmem((FEAT, 2 * DH), BF),
            vmem((SLOTS * TOK, 2 * DH), BF),
            vmem((2 * DH, SLOTS * TOK), BF),
            vmem((SLOTS, 2, TOK, DH), BF),
            vmem((HEADS, 3 * TOK, TOK), F32),
            vmem((HEADS, TOK, 2 * TOK), F32),
            vmem((HEADS, TOK, TOK), BF),
            vmem((5, TOK, TOK), F32),
            vmem((2, 8, DH, 256), BF),
            vmem((2, 8, DH, 256), BF),
            vmem((256, DH), F32),
            vmem((8, 32, DH), F32),
            sems((5,)),
            sems,
            sems,
            sems((2, 8)),
            sems((2, 8)),
            sems((10,)),
            sems((10,)),
            sems,
            sems,
            sems((4,)),
            sems((4,)),
            sems((2,)),
            sems((2,)),
            sems((8,)),
            sems((8,)),
            sems((8,)),
            sems((8,)),
            sems((8,)),
            sems((8,)),
            sems((4,)),
            sems((4,)),
            sems((2, 8)),
            sems((2, 8)),
            sems,
            sems,
        ],
        compiler_params=pltpu.CompilerParams(
            collective_id=0, has_side_effects=True, vmem_limit_bytes=48 * 1024 * 1024
        ),
    )(block_order, queries[0], keys[0], values[0], saved_output[0], d_out[0], w_out.T)
    return dq[None], dk[None], dv[None], dw


def solution(mesh):
    tokens = P("dp", "ctx", None)
    return jax.shard_map(
        per_device,
        mesh=mesh,
        in_specs=(tokens,) * 5 + (P("dp", "ctx"), P()),
        out_specs=(tokens,) * 3 + (P("dp", "ctx"),),
        check_vma=False,
    )
```

```python
import math

import jax
import jax.numpy as jnp
from jax import lax
from jax.experimental import pallas as pl
from jax.experimental.pallas import tpu as pltpu
from jax.sharding import PartitionSpec as P

DH = 128
TOK = 128
HEADS = 16
FEAT = 2048
NX, NY, NZ, NZL = 4, 4, 16, 8
SLOTS = 2 * NY
Z_OFFSETS = (1, 15, 2, 14, 3, 13, 4, 12, 5, 11, 6, 10, 7, 9, 8)
MESH = pl.DeviceIdType.MESH
KQ, VV, KO, SA, UN = 1, 3, 2, 11, 4
BF = jnp.bfloat16
F32 = jnp.float32

NT = (((1,), (1,)), ((), ()))
NN = (((1,), (0,)), ((), ()))
TN = (((0,), (0,)), ((), ()))


def dot(a, b, dims):
    return lax.dot_general(a, b, dims, preferred_element_type=F32)


def kernel(
    order_ref, q_in, k_in, v_in, saved_in, grad_in, wt_in,
    dq_ref, dk_ref, dv_ref, dw_ref,
    qb, kb, vb, sv, gb, dab, lse, delta,
    wt, ww, sb, st, dsend, probs, probs_k, ds_own, bias,
    dwp, dwb, xin, xsum, zout, zin, near_sum, quarter_out, quarter_in, mine_f, fin, turned,
    load_s, wc_s, wc_r, wz_s, wz_r, wx_s, wx_r, g_s, g_r, sa_s, sa_r, kv_s, kv_r, q_s, q_r,
    da_s, da_r, fw_s, fw_r, fo_s, fo_r, row_s, row_r, ds_s, ds_r, dn_s, dn_r, rx_s, rx_r, rz_s, rz_r, rq_s, rq_r, rf_s, rf_r,
):
    ctx = lax.axis_index("ctx")
    dp = lax.axis_index("dp")
    core = lax.rem(ctx, 2)
    x = lax.rem(lax.div(ctx, 2), NX)
    zl = lax.div(ctx, 2 * NX)
    y = lax.rem(dp, NY)
    z = lax.div(dp, NY) * NZL + zl
    n_ctx = 2 * NX * NZL
    me = 2 * y + core
    zt, zq, zr = lax.div(z, NZL), lax.div(zl, 4), lax.rem(zl, 4)

    def at(xx, yy, zz, cc):
        return {
            "ctx": lax.rem(zz, NZL) * (2 * NX) + xx * 2 + cc,
            "dp": lax.div(zz, NZL) * NY + yy,
        }

    other = at(x, y, z, 1 - core)
    after = {"ctx": lax.rem(ctx + 2, n_ctx), "dp": dp}
    before = {"ctx": lax.rem(ctx + n_ctx - 2, n_ctx), "dp": dp}
    yp, ym, yf = lax.rem(y + 1, NY), lax.rem(y + 3, NY), lax.rem(y + 2, NY)
    y_up, y_down = at(x, yp, z, core), at(x, ym, z, core)
    y_group = [(dy, dc) for dy in (1, 3, 2, 0) for dc in (0, 1) if (dy, dc) != (0, 0)]
    x_group = [(dx, dc) for dx in (1, 3, 2, 0) for dc in (0, 1) if (dx, dc) != (0, 0)]

    def y_peer(dy, dc):
        yy, cc = lax.rem(y + dy, NY), lax.rem(core + dc, 2)
        return at(x, yy, z, cc), 2 * yy + cc

    def x_peer(dx, dc):
        xx, cc = lax.rem(x + dx, NX), lax.rem(core + dc, 2)
        return at(xx, y, z, cc), xx, cc

    def send(src, dst, ssem, rsem, device):
        copy = pltpu.make_async_remote_copy(
            src_ref=src, dst_ref=dst, send_sem=ssem, recv_sem=rsem, device_id=device, device_id_type=MESH
        )
        copy.start()

    def took(ref, sem):
        pltpu.make_async_copy(ref, ref, sem).wait()

    own = pl.ds(0, TOK)
    my_rows = pl.ds(pl.multiple_of(me * TOK, TOK), TOK)
    loads = [
        pltpu.make_async_copy(grad_in, gb.at[my_rows, :], load_s.at[0]),
        pltpu.make_async_copy(saved_in, sv, load_s.at[1]),
        pltpu.make_async_copy(k_in, kb.at[own, :], load_s.at[2]),
        pltpu.make_async_copy(q_in, qb.at[own, :], load_s.at[3]),
        pltpu.make_async_copy(v_in, vb.at[own, :], load_s.at[4]),
    ]
    for load in loads:
        load.start()

    barrier = pltpu.get_barrier_semaphore()
    peers = [y_peer(*d)[0] for d in y_group] + [x_peer(*d)[0] for d in x_group if d != (0, 1)]
    peers += [at(x, y, lax.rem(z + dz, NZ), core) for dz in Z_OFFSETS] + [after, before]
    for peer in peers:
        pl.semaphore_signal(barrier, inc=1, device_id=peer, device_id_type=MESH)
    pl.semaphore_wait(barrier, len(peers))

    def w_piece(xx, zz):
        return wt.at[lax.div(zz, NZL), lax.rem(zz, NZL), xx]

    def half_lanes(cc):
        return pl.ds(pl.multiple_of(cc * DH, DH), DH)

    zh = lax.div(z, NZL)
    piece = pl.ds(pl.multiple_of(core * 32, 32), 32)
    send(wt_in.at[:, half_lanes(1 - core)], wt.at[zh, zl, x, piece], wc_s, wc_r, other)
    wt[zh, zl, x, piece] = wt_in[:, half_lanes(core)]
    def half(slot, part):
        return gb.at[pl.ds(pl.multiple_of(slot * TOK + part * 64, 64), 64), :]

    def whole(slot):
        return gb.at[pl.ds(pl.multiple_of(slot * TOK, TOK), TOK), :]

    s_up, s_down, s_far = 2 * yp + core, 2 * ym + core, 2 * yf + core
    loads[0].wait()
    send(half(me, 0), half(me, 0), g_s.at[0], g_r.at[0], y_up)
    send(half(me, 1), half(me, 1), g_s.at[1], g_r.at[1], y_down)
    send(half(me, 1), half(me, 1), g_s.at[2], g_r.at[2], y_up)
    send(half(me, 0), half(me, 0), g_s.at[3], g_r.at[3], y_down)
    send(whole(me), whole(me), g_s.at[6], g_r.at[6], other)
    took(wt_in.at[:, pl.ds(0, DH)], wc_r)
    for dz in Z_OFFSETS:
        send(w_piece(x, z), w_piece(x, z), wz_s.at[dz], wz_r.at[dz], at(x, y, lax.rem(z + dz, NZ), core))

    prev2, prev1 = pl.ds(2 * TOK, TOK), pl.ds(TOK, TOK)
    loads[2].wait()
    loads[3].wait()
    loads[4].wait()
    loads[1].wait()

    def head_lanes(h):
        return pl.ds(pl.multiple_of(h * DH, DH), DH)

    for zh in range(2):
        sb[my_rows, pl.ds(zh * DH, DH)] = sv[:, head_lanes(8 * zh + me)]

    def at_place(n):
        if n == KQ:
            send(kb.at[own, :], kb.at[prev2, :], kv_s.at[0], kv_r.at[0], after)
            send(qb.at[own, :], qb.at[prev2, :], q_s.at[0], q_r.at[0], before)
        if n == VV:
            send(vb.at[own, :], vb.at[prev2, :], kv_s.at[1], kv_r.at[1], after)
        if n == KO:
            @pl.when(core == 0)
            def _():
                send(kb.at[own, :], kb.at[prev1, :], kv_s.at[2], kv_r.at[2], other)
                send(vb.at[own, :], vb.at[prev1, :], kv_s.at[3], kv_r.at[3], other)

            @pl.when(core == 1)
            def _():
                send(qb.at[own, :], qb.at[prev1, :], q_s.at[1], q_r.at[1], other)
        if n == SA:
            for d in y_group:
                dev, slot = y_peer(*d)
                for top in range(2):
                    send(sv.at[:, head_lanes(8 * top + slot)], sb.at[my_rows, pl.ds(top * DH, DH)], sa_s, sa_r, dev)

    at_place(0)

    group = ctx
    lane = lax.broadcasted_iota(jnp.int32, (TOK, TOK), 1)
    row = lax.broadcasted_iota(jnp.int32, (TOK, TOK), 0)

    def places(g, index):
        first, second = order_ref[2 * g], order_ref[2 * g + 1]
        return jnp.where(index < 64, first * 64 + index, second * 64 + index - 64)

    def blocked(key_group, query_group):
        seen = places(key_group, row) <= places(query_group, lane)
        return jnp.where(seen, 0.0, -1e30).astype(F32)

    def shifted(by):
        return lax.rem(group + n_ctx + by, n_ctx)

    bias[0] = blocked(group, group)
    bias[1] = blocked(shifted(-1), group)
    bias[2] = blocked(shifted(-2), group)
    bias[3] = blocked(group, shifted(1))
    bias[4] = blocked(group, shifted(2))
    scale = 1.0 / math.sqrt(DH)

    def own_scores(i, carry):
        lanes = head_lanes(8 * lax.rem(i, 2) + lax.div(i, 2))
        probs[i, 0:TOK] = dot(kb[own, lanes], qb[own, lanes], NT) * scale + bias[0]
        return carry

    lax.fori_loop(0, HEADS, own_scores, 0, unroll=UN)

    def z_peer(dz):
        return at(x, y, lax.rem(z + dz, NZ), core)

    def rest_of(d):
        return lax.rem(zr + d, 4)

    def w_across(zz):
        for i, dx in enumerate((1, 3, 2)):
            send(w_piece(x, zz), w_piece(x, zz), wx_s, wx_r, at(lax.rem(x + dx, NX), y, z, core))

    w_across(z)
    for i, dz in enumerate(Z_OFFSETS):
        zz = lax.rem(z + dz, NZ)
        took(w_piece(x, zz), wz_r.at[NZ - dz])
        w_across(zz)
        if KQ == 1 and i % 2 == 0:
            part = i // 2 * 16
            send(kb.at[pl.ds(part, 16), :], kb.at[pl.ds(2 * TOK + part, 16), :], kv_s.at[0], kv_r.at[0], after)
            send(qb.at[pl.ds(part, 16), :], qb.at[pl.ds(2 * TOK + part, 16), :], q_s.at[0], q_r.at[0], before)
        if i == 5:
            took(half(s_down, 0), g_r.at[0])
            send(half(s_down, 0), half(s_down, 0), g_s.at[4], g_r.at[4], y_up)
            took(half(s_up, 1), g_r.at[1])
            send(half(s_up, 1), half(s_up, 1), g_s.at[5], g_r.at[5], y_down)
            at_place(11)
    at_place(2)
    took(half(s_down, 1), g_r.at[2])
    send(whole(s_down), whole(s_down), g_s.at[7], g_r.at[7], other)
    took(half(s_up, 0), g_r.at[3])
    send(whole(s_up), whole(s_up), g_s.at[8], g_r.at[8], other)
    took(wt.at[:, :, pl.ds(0, 3)], wx_r)
    at_place(3)

    took(half(s_far, 0), g_r.at[4])
    took(half(s_far, 1), g_r.at[5])
    send(whole(s_far), whole(s_far), g_s.at[9], g_r.at[9], other)
    for i in range(6, 10):
        took(whole(me), g_r.at[i])

    ww[:, 0:DH] = wt[0].reshape(FEAT, DH)
    ww[:, DH:] = wt[1].reshape(FEAT, DH)
    def attn_step(j, carry):
        dy = 2 - j + 3 * lax.div(j, 2) - 2 * lax.div(j, 3)
        yy = lax.rem(y + dy, NY)
        rows = pl.ds(pl.multiple_of(yy * 256, 256), 256)
        part = dot(gb[rows, :], ww[...], NN).astype(BF)
        for cc in range(2):
            slot = 2 * yy + cc
            for top in range(2):
                dsend[slot, top] = part[cc * TOK : (cc + 1) * TOK, top * DH : (top + 1) * DH]

            @pl.when(slot != me)
            def _():
                send(
                    dsend.at[slot], dab.at[pl.ds(2 * me, 2), own, :], da_s.at[slot], da_r.at[me],
                    at(x, yy, z, cc),
                )
        return carry

    lax.fori_loop(0, 4, attn_step, 0)
    for top in range(2):
        dab[2 * me + top, 0:TOK, :] = dsend[me, top]

    at_place(4)
    took(sb.at[pl.ds(0, 896), :], sa_r)
    st[...] = sb[...].astype(F32).T.astype(BF)

    def part_lanes(part):
        return pl.ds(part * 1024, 1024)

    def partial_sums(low, carry):
        lanes = pl.ds(pl.multiple_of(low * 256, 256), 256)
        sums = dot(st[...], gb[:, lanes], NN).reshape(2, NX, 32, 256)
        dwp[:, :, :, lanes] = sums
        dwb[:, :, :, lanes] = sums.astype(BF)
        return carry

    for part in range(2):
        lax.fori_loop(4 * part, 4 * part + 4, partial_sums, 0)
        for dx in (1, 3, 2):
            xx = lax.rem(x + dx, NX)
            send(
                dwb.at[:, xx, :, part_lanes(part)], xin.at[part, dx], rx_s.at[part, dx], rx_r.at[part, dx],
                at(xx, y, z, core),
            )

    at_place(5)

    def over_z(part):
        sums = dwp[:, x, :, part_lanes(part)]
        for dx in (1, 3, 2):
            took(xin.at[part, dx], rx_r.at[part, dx])
            sums = sums + xin[part, dx].astype(F32)
        for top in range(2):
            for rest in range(4):
                block = sums[top, :, rest * 256 : (rest + 1) * 256]
                xsum[rest, part, top] = block
                zout[rest, part, top] = block.astype(BF)
        send(zout.at[rest_of(1), part], zin.at[0, part], rz_s.at[part, 0], rz_r.at[part, 0], z_peer(1))
        send(zout.at[rest_of(3), part], zin.at[1, part], rz_s.at[part, 1], rz_r.at[part, 1], z_peer(15))
        send(zout.at[rest_of(2), part, 0], zin.at[2, part, 0], rz_s.at[part, 2], rz_r.at[part, 2], z_peer(2))
        send(zout.at[rest_of(2), part, 1], zin.at[2, part, 1], rz_s.at[part, 3], rz_r.at[part, 3], z_peer(14))

    def over_quarters(part):
        for i in range(2):
            took(zin.at[i, part], rz_r.at[part, i])
            took(zin.at[2, part, i], rz_r.at[part, 2 + i])
        sums = xsum[zr, part]
        for i in range(3):
            sums = sums + zin[i, part].astype(F32)
        near_sum[part] = sums
        quarter_out[part] = sums.astype(BF)
        for top in range(2):
            @pl.when((zq != part) | (zt != top))
            def _():
                send(
                    quarter_out.at[part, top], quarter_in.at[zq, zt], rq_s.at[part, top], rq_r,
                    at(x, y, top * NZL + part * 4 + zr, core),
                )

    took(kb.at[prev2, :], kv_r.at[0])
    took(qb.at[prev2, :], q_r.at[0])

    @pl.when(core == 1)
    def _():
        send(kb.at[prev2, :], kb.at[prev1, :], kv_s.at[2], kv_r.at[2], other)

    @pl.when(core == 0)
    def _():
        send(qb.at[prev2, :], qb.at[prev1, :], q_s.at[1], q_r.at[1], other)

    took(kb.at[prev1, :], kv_r.at[2])

    def score_head(i, carry):
        h = 8 * lax.rem(i, 2) + lax.div(i, 2)
        lanes = head_lanes(h)
        s = dot(kb[TOK:, lanes], qb[own, lanes], NT) * scale + bias[1:3].reshape(2 * TOK, TOK)
        s = jnp.concatenate([probs[i, 0:TOK], s], axis=0)
        top = jnp.max(s, axis=0, keepdims=True)
        e = jnp.exp(s - top)
        total = jnp.sum(e, axis=0, keepdims=True)
        probs[i] = e * (1.0 / total)
        lse[0, i] = top + jnp.log(total)
        return carry

    lax.fori_loop(0, HEADS, score_head, 0, unroll=UN)

    near, far = pl.ds(TOK, TOK), pl.ds(2 * TOK, TOK)
    send(lse.at[0], lse.at[2], row_s.at[0], row_r.at[0], before)

    @pl.when(core == 1)
    def _():
        send(lse.at[0], lse.at[1], row_s.at[1], row_r.at[1], other)

    def chunk(slot, rows):
        return dab.at[pl.ds(2 * slot, 2), rows, :]

    ones = jnp.ones((8, DH), BF)

    def deltas(slot, which):
        return delta.at[which, pl.ds(2 * slot, 2)]

    def pass_on(slot):
        @pl.when(slot != me)
        def _():
            took(chunk(slot, own), da_r.at[slot])

        send(chunk(slot, own), chunk(slot, far), fw_s.at[slot], fw_r.at[slot], before)

        @pl.when(core == 1)
        def _():
            send(chunk(slot, own), chunk(slot, near), fo_s.at[slot], fo_r.at[slot], other)

        for zh in range(2):
            i = 2 * slot + zh
            prod = dab[i, 0:TOK, :].astype(F32) * sv[:, head_lanes(8 * zh + slot)].astype(F32)
            high = prod.astype(BF)
            low = (prod - high.astype(F32)).astype(BF)
            sums = dot(ones, high, NT) + dot(ones, low, NT)
            delta[0, i] = sums[0:1]
        send(deltas(slot, 0), deltas(slot, 2), ds_s.at[slot], ds_r.at[slot], before)

        @pl.when(core == 1)
        def _():
            send(deltas(slot, 0), deltas(slot, 1), dn_s.at[slot], dn_r.at[slot], other)

    def turn(j):
        dy = lax.div(j, 2)
        dy = dy + lax.div(dy, 2) - 2 * lax.div(dy, 3)
        return 2 * lax.rem(y + dy, NY) + lax.rem(j, 2)

    def pass_step(j, carry):
        pass_on(turn(j))
        return carry

    lax.fori_loop(0, SLOTS, pass_step, 0)
    at_place(6)

    over_z(0)

    took(qb.at[near, :], q_r.at[1])
    took(lse.at[2], row_r.at[0])

    @pl.when(core == 0)
    def _():
        send(lse.at[2], lse.at[1], row_s.at[1], row_r.at[1], other)

    took(lse.at[1], row_r.at[1])

    def later_head(i, carry):
        h = 8 * lax.rem(i, 2) + lax.div(i, 2)
        lanes = head_lanes(h)
        s = dot(kb[own, lanes], qb[TOK:, lanes], NT) * scale
        s = s + jnp.concatenate([bias[3], bias[4]], axis=1)
        probs_k[i] = jnp.exp(s - jnp.concatenate([lse[1, i], lse[2, i]], axis=1))
        return carry

    lax.fori_loop(0, HEADS, later_head, 0, unroll=UN)
    over_z(1)
    over_quarters(0)

    took(vb.at[prev2, :], kv_r.at[1])

    @pl.when(core == 1)
    def _():
        send(vb.at[prev2, :], vb.at[prev1, :], kv_s.at[3], kv_r.at[3], other)

    took(vb.at[prev1, :], kv_r.at[3])

    def own_head(i, carry):
        h = 8 * lax.rem(i, 2) + lax.div(i, 2)
        lanes = head_lanes(h)
        dprobs = dot(vb[:, lanes], dab[i, 0:TOK, :], NT)
        ds = (probs[i] * (dprobs - delta[0, i])).astype(BF)
        ds_own[i] = ds[0:TOK]
        dq_ref[:, lanes] = (dot(ds, kb[:, lanes], TN) * scale).astype(BF)
        return carry

    lax.fori_loop(0, HEADS, own_head, 0, unroll=UN)
    over_quarters(1)

    def key_head(i, carry):
        h = 8 * lax.rem(i, 2) + lax.div(i, 2)
        lanes = head_lanes(h)
        later = dab[i, TOK:, :]
        p = probs_k[i]
        dprobs = dot(vb[own, lanes], later, NT)
        ds = (p * (dprobs - jnp.concatenate([delta[1, i], delta[2, i]], axis=1))).astype(BF)
        dkey = dot(ds_own[i], qb[own, lanes], NN) + dot(ds, qb[TOK:, lanes], NN)
        dk_ref[:, lanes] = (dkey * scale).astype(BF)
        dval = dot(probs[i, 0:TOK, :].astype(BF), dab[i, 0:TOK, :], NN) + dot(p.astype(BF), later, NN)
        dv_ref[:, lanes] = dval.astype(BF)
        return carry


    def d_wo_sum():
        quarter_in[zq, zt] = jnp.zeros((32, 256), BF)
        took(zin.at[pl.ds(0, 3), 0, 0], rq_r)
        total = near_sum[zq, zt]
        for i in range(4):
            total = total + quarter_in[i // 2, i % 2].astype(F32)
        grad_scale = 1.0 / math.sqrt(8 * n_ctx * TOK)
        mine_f[...] = total * grad_scale
        for d in x_group:
            send(mine_f, fin.at[core * NX + x], rf_s, rf_r, x_peer(*d)[0])
        fin[core * NX + x] = mine_f[...]

    def from_next(slot):
        took(chunk(slot, far), fw_r.at[slot])
        took(deltas(slot, 2), ds_r.at[slot])

        @pl.when(core == 0)
        def _():
            send(chunk(slot, far), chunk(slot, near), fo_s.at[slot], fo_r.at[slot], other)
            send(deltas(slot, 2), deltas(slot, 1), dn_s.at[slot], dn_r.at[slot], other)

    def from_other(slot):
        took(chunk(slot, near), fo_r.at[slot])
        took(deltas(slot, 1), dn_r.at[slot])
        lax.fori_loop(2 * slot, 2 * slot + 2, key_head, 0)

    def key_step(j, carry):
        from_next(turn(j))
        from_other(turn(j - 1))
        return carry

    from_next(turn(0))
    lax.fori_loop(1, 6, key_step, 0)
    d_wo_sum()
    lax.fori_loop(6, SLOTS, key_step, 0)
    from_other(turn(SLOTS - 1))

    took(fin.at[pl.ds(0, 7)], rf_r)
    turned[...] = fin[...].reshape(2 * DH, 256).T
    dw_ref[...] = turned[pl.ds(pl.multiple_of((2 * x + core) * 32, 32), 32), :]

    took(wt_in.at[:, pl.ds(0, DH)], wc_s)
    for dz in Z_OFFSETS:
        took(w_piece(x, z), wz_s.at[dz])
    took(wt.at[:, :, pl.ds(0, 3)], wx_s)
    for part in range(2):
        for dx in (1, 3, 2):
            took(xin.at[part, dx], rx_s.at[part, dx])
    for part in range(2):
        for i in range(2):
            took(zin.at[i, part], rz_s.at[part, i])
            took(zin.at[2, part, i], rz_s.at[part, 2 + i])
        for top in range(2):
            @pl.when((zq != part) | (zt != top))
            def _():
                took(quarter_out.at[part, top], rq_s.at[part, top])
    took(fin.at[pl.ds(0, 7)], rf_s)
    for i in range(6):
        took(half(me, 0), g_s.at[i])
    for i in range(6, 10):
        took(whole(me), g_s.at[i])
    took(sb.at[pl.ds(0, 896), :], sa_s)
    for i in range(4):
        took(kb.at[own, :], kv_s.at[i])
    for i in range(2):
        took(lse.at[0], row_s.at[i])
    for i in range(2):
        took(qb.at[own, :], q_s.at[i])
    for slot in range(SLOTS):
        @pl.when(slot != me)
        def _():
            took(dsend.at[0], da_s.at[slot])

    for slot in range(SLOTS):
        took(chunk(slot, own), fw_s.at[slot])
        took(chunk(slot, own), fo_s.at[slot])
        took(deltas(slot, 0), ds_s.at[slot])
        took(deltas(slot, 0), dn_s.at[slot])


def per_device(queries, keys, values, saved_output, d_out, w_out, block_order):
    sems = pltpu.SemaphoreType.DMA
    vmem = pltpu.VMEM
    tokens = jax.ShapeDtypeStruct((TOK, FEAT), BF)
    anywhere = pl.BlockSpec(memory_space=pltpu.HBM)
    inside = pl.BlockSpec(memory_space=pltpu.VMEM)
    dq, dk, dv, dw = pl.pallas_call(
        kernel,
        out_shape=(tokens, tokens, tokens, jax.ShapeDtypeStruct((32, 256), F32)),
        in_specs=[pl.BlockSpec(memory_space=pltpu.SMEM)] + [anywhere] * 5 + [inside],
        out_specs=(inside,) * 4,
        scratch_shapes=[
            vmem((3 * TOK, FEAT), BF),
            vmem((3 * TOK, FEAT), BF),
            vmem((3 * TOK, FEAT), BF),
            vmem((TOK, FEAT), BF),
            vmem((SLOTS * TOK, FEAT), BF),
            vmem((HEADS, 3 * TOK, DH), BF),
            vmem((3, HEADS, 1, TOK), F32),
            vmem((3, HEADS, 1, TOK), F32),
            vmem((2, NZL, NX, 64, DH), BF),
            vmem((FEAT, 2 * DH), BF),
            vmem((SLOTS * TOK, 2 * DH), BF),
            vmem((2 * DH, SLOTS * TOK), BF),
            vmem((SLOTS, 2, TOK, DH), BF),
            vmem((HEADS, 3 * TOK, TOK), F32),
            vmem((HEADS, TOK, 2 * TOK), F32),
            vmem((HEADS, TOK, TOK), BF),
            vmem((5, TOK, TOK), F32),
            vmem((2, NX, 32, FEAT), F32),
            vmem((2, NX, 32, FEAT), BF),
            vmem((2, NX, 2, 32, 1024), BF),
            vmem((4, 2, 2, 32, 256), F32),
            vmem((4, 2, 2, 32, 256), BF),
            vmem((3, 2, 2, 32, 256), BF),
            vmem((2, 2, 32, 256), F32),
            vmem((2, 2, 32, 256), BF),
            vmem((2, 2, 32, 256), BF),
            vmem((32, 256), F32),
            vmem((2 * NX, 32, 256), F32),
            vmem((256, 2 * DH), F32),
            sems((5,)),
            sems,
            sems,
            sems((NZ,)),
            sems((NZ,)),
            sems,
            sems,
            sems((10,)),
            sems((10,)),
            sems,
            sems,
            sems((4,)),
            sems((4,)),
            sems((2,)),
            sems((2,)),
            sems((8,)),
            sems((8,)),
            sems((8,)),
            sems((8,)),
            sems((8,)),
            sems((8,)),
            sems((2,)),
            sems((2,)),
            sems((8,)),
            sems((8,)),
            sems((8,)),
            sems((8,)),
            sems((2, NX)),
            sems((2, NX)),
            sems((2, 4)),
            sems((2, 4)),
            sems((2, 2)),
            sems,
            sems,
            sems,
        ],
        compiler_params=pltpu.CompilerParams(
            collective_id=0, has_side_effects=True, vmem_limit_bytes=60 * 1024 * 1024
        ),
    )(block_order, queries[0], keys[0], values[0], saved_output[0], d_out[0], w_out.T)
    return dq[None], dk[None], dv[None], dw.T


def solution(mesh):
    tokens = P("dp", "ctx", None)
    return jax.shard_map(
        per_device,
        mesh=mesh,
        in_specs=(tokens,) * 5 + (P("dp", "ctx"), P()),
        out_specs=(tokens,) * 3 + (P("dp", "ctx"),),
        check_vma=False,
    )
```

```python
import math

import jax
import jax.numpy as jnp
from jax import lax
from jax.experimental import pallas as pl
from jax.experimental.pallas import tpu as pltpu
from jax.sharding import PartitionSpec as P

DH = 128
TOK = 128
HEADS = 16
FEAT = 2048
NX, NY, NZ, NZL = 4, 4, 16, 8
SLOTS = 2 * NY
Z_OFFSETS = (1, 15, 2, 14, 3, 13, 4, 12, 5, 11, 6, 10, 7, 9, 8)
MESH = pl.DeviceIdType.MESH
UNROLL = 4
BF = jnp.bfloat16
F32 = jnp.float32

NT = (((1,), (1,)), ((), ()))
NN = (((1,), (0,)), ((), ()))
TN = (((0,), (0,)), ((), ()))


def dot(a, b, dims):
    return lax.dot_general(a, b, dims, preferred_element_type=F32)


def kernel(
    order_ref, q_in, k_in, v_in, saved_in, grad_in, wt_in,
    dq_ref, dk_ref, dv_ref, dw_ref,
    qb, kb, vb, sv, gb, dab, lse, delta,
    wt, ww, sb, st, dsend, probs, probs_k, ds_own, bias,
    dwp, dwb, xin, xsum, zout, zin, near_sum, quarter_out, quarter_in, mine_f, fin, turned,
    load_s, wc_s, wc_r, wz_s, wz_r, wx_s, wx_r, g_s, g_r, sa_s, sa_r, kv_s, kv_r, q_s, q_r,
    da_s, da_r, fw_s, fw_r, fo_s, fo_r, row_s, row_r, ds_s, ds_r, dn_s, dn_r, rx_s, rx_r, rz_s, rz_r, rq_s, rq_r, rf_s, rf_r,
):
    ctx = lax.axis_index("ctx")
    dp = lax.axis_index("dp")
    core = lax.rem(ctx, 2)
    x = lax.rem(lax.div(ctx, 2), NX)
    zl = lax.div(ctx, 2 * NX)
    y = lax.rem(dp, NY)
    z = lax.div(dp, NY) * NZL + zl
    n_ctx = 2 * NX * NZL
    me = 2 * y + core
    zt, zq, zr = lax.div(z, NZL), lax.div(zl, 4), lax.rem(zl, 4)

    def at(xx, yy, zz, cc):
        return {
            "ctx": lax.rem(zz, NZL) * (2 * NX) + xx * 2 + cc,
            "dp": lax.div(zz, NZL) * NY + yy,
        }

    other = at(x, y, z, 1 - core)
    after = {"ctx": lax.rem(ctx + 2, n_ctx), "dp": dp}
    before = {"ctx": lax.rem(ctx + n_ctx - 2, n_ctx), "dp": dp}
    yp, ym, yf = lax.rem(y + 1, NY), lax.rem(y + 3, NY), lax.rem(y + 2, NY)
    y_up, y_down = at(x, yp, z, core), at(x, ym, z, core)
    y_group = [(dy, dc) for dy in (1, 3, 2, 0) for dc in (0, 1) if (dy, dc) != (0, 0)]
    x_group = [(dx, dc) for dx in (1, 3, 2, 0) for dc in (0, 1) if (dx, dc) != (0, 0)]

    def y_peer(dy, dc):
        yy, cc = lax.rem(y + dy, NY), lax.rem(core + dc, 2)
        return at(x, yy, z, cc), 2 * yy + cc

    def x_peer(dx, dc):
        xx, cc = lax.rem(x + dx, NX), lax.rem(core + dc, 2)
        return at(xx, y, z, cc), xx, cc

    def send(src, dst, ssem, rsem, device):
        copy = pltpu.make_async_remote_copy(
            src_ref=src, dst_ref=dst, send_sem=ssem, recv_sem=rsem, device_id=device, device_id_type=MESH
        )
        copy.start()

    def took(ref, sem):
        pltpu.make_async_copy(ref, ref, sem).wait()

    own = pl.ds(0, TOK)
    my_rows = pl.ds(pl.multiple_of(me * TOK, TOK), TOK)
    loads = [
        pltpu.make_async_copy(grad_in, gb.at[my_rows, :], load_s.at[0]),
        pltpu.make_async_copy(saved_in, sv, load_s.at[1]),
        pltpu.make_async_copy(k_in, kb.at[own, :], load_s.at[2]),
        pltpu.make_async_copy(q_in, qb.at[own, :], load_s.at[3]),
        pltpu.make_async_copy(v_in, vb.at[own, :], load_s.at[4]),
    ]
    for load in loads:
        load.start()

    barrier = pltpu.get_barrier_semaphore()
    peers = [y_peer(*d)[0] for d in y_group] + [x_peer(*d)[0] for d in x_group if d != (0, 1)]
    peers += [at(x, y, lax.rem(z + dz, NZ), core) for dz in Z_OFFSETS] + [after, before]
    for peer in peers:
        pl.semaphore_signal(barrier, inc=1, device_id=peer, device_id_type=MESH)
    pl.semaphore_wait(barrier, len(peers))

    def w_piece(xx, zz):
        return wt.at[lax.div(zz, NZL), lax.rem(zz, NZL), xx]

    def half_lanes(cc):
        return pl.ds(pl.multiple_of(cc * DH, DH), DH)

    zh = lax.div(z, NZL)
    piece = pl.ds(pl.multiple_of(core * 32, 32), 32)
    send(wt_in.at[:, half_lanes(1 - core)], wt.at[zh, zl, x, piece], wc_s, wc_r, other)
    wt[zh, zl, x, piece] = wt_in[:, half_lanes(core)]
    def half(slot, part):
        return gb.at[pl.ds(pl.multiple_of(slot * TOK + part * 64, 64), 64), :]

    def whole(slot):
        return gb.at[pl.ds(pl.multiple_of(slot * TOK, TOK), TOK), :]

    s_up, s_down, s_far = 2 * yp + core, 2 * ym + core, 2 * yf + core
    loads[0].wait()
    send(half(me, 0), half(me, 0), g_s.at[0], g_r.at[0], y_up)
    send(half(me, 1), half(me, 1), g_s.at[1], g_r.at[1], y_down)
    send(half(me, 1), half(me, 1), g_s.at[2], g_r.at[2], y_up)
    send(half(me, 0), half(me, 0), g_s.at[3], g_r.at[3], y_down)
    send(whole(me), whole(me), g_s.at[6], g_r.at[6], other)
    took(wt_in.at[:, pl.ds(0, DH)], wc_r)
    for dz in Z_OFFSETS:
        send(w_piece(x, z), w_piece(x, z), wz_s.at[dz], wz_r.at[dz], at(x, y, lax.rem(z + dz, NZ), core))

    prev2, prev1 = pl.ds(2 * TOK, TOK), pl.ds(TOK, TOK)
    loads[2].wait()
    loads[3].wait()
    loads[4].wait()
    loads[1].wait()

    def head_lanes(h):
        return pl.ds(pl.multiple_of(h * DH, DH), DH)

    for zh in range(2):
        sb[my_rows, pl.ds(zh * DH, DH)] = sv[:, head_lanes(8 * zh + me)]

    def keys_and_queries(first, rows):
        def part(start):
            return pl.ds(start + first, rows)

        @pl.when(x != NX - 1)
        def _():
            send(kb.at[part(0), :], kb.at[part(2 * TOK), :], kv_s.at[0], kv_r.at[0], after)

        @pl.when(x != 0)
        def _():
            send(qb.at[part(0), :], qb.at[part(2 * TOK), :], q_s.at[0], q_r.at[0], before)

    keys_and_queries(0, 32)

    @pl.when(x == NX - 1)
    def _():
        send(kb.at[own, :], kb.at[prev2, :], kv_s.at[0], kv_r.at[0], after)

    @pl.when(x == 0)
    def _():
        send(qb.at[own, :], qb.at[prev2, :], q_s.at[0], q_r.at[0], before)


    group = ctx
    lane = lax.broadcasted_iota(jnp.int32, (TOK, TOK), 1)
    row = lax.broadcasted_iota(jnp.int32, (TOK, TOK), 0)

    def places(g, index):
        first, second = order_ref[2 * g], order_ref[2 * g + 1]
        return jnp.where(index < 64, first * 64 + index, second * 64 + index - 64)

    def blocked(key_group, query_group):
        seen = places(key_group, row) <= places(query_group, lane)
        return jnp.where(seen, 0.0, -1e30).astype(F32)

    def shifted(by):
        return lax.rem(group + n_ctx + by, n_ctx)

    bias[0] = blocked(group, group)
    bias[1] = blocked(shifted(-1), group)
    bias[2] = blocked(shifted(-2), group)
    bias[3] = blocked(group, shifted(1))
    bias[4] = blocked(group, shifted(2))
    scale = 1.0 / math.sqrt(DH)

    def own_scores(i, carry):
        lanes = head_lanes(8 * lax.rem(i, 2) + lax.div(i, 2))
        probs[i, 0:TOK] = dot(kb[own, lanes], qb[own, lanes], NT) * scale + bias[0]
        return carry

    lax.fori_loop(0, HEADS, own_scores, 0, unroll=UNROLL)

    def z_peer(dz):
        return at(x, y, lax.rem(z + dz, NZ), core)

    def rest_of(d):
        return lax.rem(zr + d, 4)

    def w_across(zz):
        for i, dx in enumerate((1, 3, 2)):
            send(w_piece(x, zz), w_piece(x, zz), wx_s, wx_r, at(lax.rem(x + dx, NX), y, z, core))

    w_across(z)
    for i, dz in enumerate(Z_OFFSETS):
        zz = lax.rem(z + dz, NZ)
        took(w_piece(x, zz), wz_r.at[NZ - dz])
        w_across(zz)
        if i == 5:
            took(half(s_down, 0), g_r.at[0])
            send(half(s_down, 0), half(s_down, 0), g_s.at[4], g_r.at[4], y_up)
            took(half(s_up, 1), g_r.at[1])
            send(half(s_up, 1), half(s_up, 1), g_s.at[5], g_r.at[5], y_down)
            for d in y_group:
                dev, slot = y_peer(*d)
                for top in range(2):
                    send(sv.at[:, head_lanes(8 * top + slot)], sb.at[my_rows, pl.ds(top * DH, DH)], sa_s, sa_r, dev)
    keys_and_queries(32, 96)

    @pl.when(core == 0)
    def _():
        send(kb.at[own, :], kb.at[prev1, :], kv_s.at[2], kv_r.at[2], other)
        send(vb.at[own, :], vb.at[prev1, :], kv_s.at[3], kv_r.at[3], other)

    @pl.when(core == 1)
    def _():
        send(qb.at[own, :], qb.at[prev1, :], q_s.at[1], q_r.at[1], other)

    took(half(s_down, 1), g_r.at[2])
    send(whole(s_down), whole(s_down), g_s.at[7], g_r.at[7], other)
    took(half(s_up, 0), g_r.at[3])
    send(whole(s_up), whole(s_up), g_s.at[8], g_r.at[8], other)
    took(wt.at[:, :, pl.ds(0, 3)], wx_r)
    send(vb.at[own, :], vb.at[prev2, :], kv_s.at[1], kv_r.at[1], after)

    took(half(s_far, 0), g_r.at[4])
    took(half(s_far, 1), g_r.at[5])
    send(whole(s_far), whole(s_far), g_s.at[9], g_r.at[9], other)
    for i in range(6, 10):
        took(whole(me), g_r.at[i])

    ww[:, 0:DH] = wt[0].reshape(FEAT, DH)
    ww[:, DH:] = wt[1].reshape(FEAT, DH)
    def attn_step(j, carry):
        dy = 2 - j + 3 * lax.div(j, 2) - 2 * lax.div(j, 3)
        yy = lax.rem(y + dy, NY)
        rows = pl.ds(pl.multiple_of(yy * 256, 256), 256)
        part = dot(gb[rows, :], ww[...], NN).astype(BF)
        for cc in range(2):
            slot = 2 * yy + cc
            for top in range(2):
                dsend[slot, top] = part[cc * TOK : (cc + 1) * TOK, top * DH : (top + 1) * DH]

            @pl.when(slot != me)
            def _():
                send(
                    dsend.at[slot], dab.at[pl.ds(2 * me, 2), own, :], da_s.at[slot], da_r.at[me],
                    at(x, yy, z, cc),
                )
        return carry

    lax.fori_loop(0, 4, attn_step, 0)
    for top in range(2):
        dab[2 * me + top, 0:TOK, :] = dsend[me, top]

    took(sb.at[pl.ds(0, 896), :], sa_r)
    st[...] = sb[...].astype(F32).T.astype(BF)

    def part_lanes(part):
        return pl.ds(part * 1024, 1024)

    def partial_sums(low, carry):
        lanes = pl.ds(pl.multiple_of(low * 256, 256), 256)
        sums = dot(st[...], gb[:, lanes], NN).reshape(2, NX, 32, 256)
        dwp[:, :, :, lanes] = sums
        dwb[:, :, :, lanes] = sums.astype(BF)
        return carry

    for part in range(2):
        lax.fori_loop(4 * part, 4 * part + 4, partial_sums, 0)
        for dx in (1, 3, 2):
            xx = lax.rem(x + dx, NX)
            send(
                dwb.at[:, xx, :, part_lanes(part)], xin.at[part, dx], rx_s.at[part, dx], rx_r.at[part, dx],
                at(xx, y, z, core),
            )


    def over_z(part):
        sums = dwp[:, x, :, part_lanes(part)]
        for dx in (1, 3, 2):
            took(xin.at[part, dx], rx_r.at[part, dx])
            sums = sums + xin[part, dx].astype(F32)
        for top in range(2):
            for rest in range(4):
                block = sums[top, :, rest * 256 : (rest + 1) * 256]
                xsum[rest, part, top] = block
                zout[rest, part, top] = block.astype(BF)
        send(zout.at[rest_of(1), part], zin.at[0, part], rz_s.at[part, 0], rz_r.at[part, 0], z_peer(1))
        send(zout.at[rest_of(3), part], zin.at[1, part], rz_s.at[part, 1], rz_r.at[part, 1], z_peer(15))
        send(zout.at[rest_of(2), part, 0], zin.at[2, part, 0], rz_s.at[part, 2], rz_r.at[part, 2], z_peer(2))
        send(zout.at[rest_of(2), part, 1], zin.at[2, part, 1], rz_s.at[part, 3], rz_r.at[part, 3], z_peer(14))

    def over_quarters(part):
        for i in range(2):
            took(zin.at[i, part], rz_r.at[part, i])
            took(zin.at[2, part, i], rz_r.at[part, 2 + i])
        sums = xsum[zr, part]
        for i in range(3):
            sums = sums + zin[i, part].astype(F32)
        near_sum[part] = sums
        quarter_out[part] = sums.astype(BF)
        for top in range(2):
            @pl.when((zq != part) | (zt != top))
            def _():
                send(
                    quarter_out.at[part, top], quarter_in.at[zq, zt], rq_s.at[part, top], rq_r,
                    at(x, y, top * NZL + part * 4 + zr, core),
                )

    took(kb.at[prev2, :], kv_r.at[0])
    took(qb.at[prev2, :], q_r.at[0])

    @pl.when(core == 1)
    def _():
        send(kb.at[prev2, :], kb.at[prev1, :], kv_s.at[2], kv_r.at[2], other)

    @pl.when(core == 0)
    def _():
        send(qb.at[prev2, :], qb.at[prev1, :], q_s.at[1], q_r.at[1], other)

    took(kb.at[prev1, :], kv_r.at[2])

    def score_head(i, carry):
        h = 8 * lax.rem(i, 2) + lax.div(i, 2)
        lanes = head_lanes(h)
        s = dot(kb[TOK:, lanes], qb[own, lanes], NT) * scale + bias[1:3].reshape(2 * TOK, TOK)
        s = jnp.concatenate([probs[i, 0:TOK], s], axis=0)
        top = jnp.max(s, axis=0, keepdims=True)
        e = jnp.exp(s - top)
        total = jnp.sum(e, axis=0, keepdims=True)
        probs[i] = e * (1.0 / total)
        lse[0, i] = top + jnp.log(total)
        return carry

    lax.fori_loop(0, HEADS, score_head, 0, unroll=UNROLL)

    near, far = pl.ds(TOK, TOK), pl.ds(2 * TOK, TOK)
    send(lse.at[0], lse.at[2], row_s.at[0], row_r.at[0], before)

    @pl.when(core == 1)
    def _():
        send(lse.at[0], lse.at[1], row_s.at[1], row_r.at[1], other)

    def chunk(slot, rows):
        return dab.at[pl.ds(2 * slot, 2), rows, :]

    ones = jnp.ones((8, DH), BF)

    def deltas(slot, which):
        return delta.at[which, pl.ds(2 * slot, 2)]

    def pass_on(slot):
        @pl.when(slot != me)
        def _():
            took(chunk(slot, own), da_r.at[slot])

        send(chunk(slot, own), chunk(slot, far), fw_s.at[slot], fw_r.at[slot], before)

        @pl.when(core == 1)
        def _():
            send(chunk(slot, own), chunk(slot, near), fo_s.at[slot], fo_r.at[slot], other)

        for zh in range(2):
            i = 2 * slot + zh
            prod = dab[i, 0:TOK, :].astype(F32) * sv[:, head_lanes(8 * zh + slot)].astype(F32)
            high = prod.astype(BF)
            low = (prod - high.astype(F32)).astype(BF)
            sums = dot(ones, high, NT) + dot(ones, low, NT)
            delta[0, i] = sums[0:1]
        send(deltas(slot, 0), deltas(slot, 2), ds_s.at[slot], ds_r.at[slot], before)

        @pl.when(core == 1)
        def _():
            send(deltas(slot, 0), deltas(slot, 1), dn_s.at[slot], dn_r.at[slot], other)

    def turn(j):
        dy = lax.div(j, 2)
        dy = dy + lax.div(dy, 2) - 2 * lax.div(dy, 3)
        return 2 * lax.rem(y + dy, NY) + lax.rem(j, 2)

    def pass_step(j, carry):
        pass_on(turn(j))
        return carry

    lax.fori_loop(0, SLOTS, pass_step, 0)

    over_z(0)

    took(qb.at[near, :], q_r.at[1])
    took(lse.at[2], row_r.at[0])

    @pl.when(core == 0)
    def _():
        send(lse.at[2], lse.at[1], row_s.at[1], row_r.at[1], other)

    took(lse.at[1], row_r.at[1])

    def later_head(i, carry):
        h = 8 * lax.rem(i, 2) + lax.div(i, 2)
        lanes = head_lanes(h)
        s = dot(kb[own, lanes], qb[TOK:, lanes], NT) * scale
        s = s + jnp.concatenate([bias[3], bias[4]], axis=1)
        probs_k[i] = jnp.exp(s - jnp.concatenate([lse[1, i], lse[2, i]], axis=1))
        return carry

    lax.fori_loop(0, HEADS, later_head, 0, unroll=UNROLL)
    over_z(1)
    over_quarters(0)

    took(vb.at[prev2, :], kv_r.at[1])

    @pl.when(core == 1)
    def _():
        send(vb.at[prev2, :], vb.at[prev1, :], kv_s.at[3], kv_r.at[3], other)

    took(vb.at[prev1, :], kv_r.at[3])

    def own_head(i, carry):
        h = 8 * lax.rem(i, 2) + lax.div(i, 2)
        lanes = head_lanes(h)
        dprobs = dot(vb[:, lanes], dab[i, 0:TOK, :], NT)
        ds = (probs[i] * (dprobs - delta[0, i])).astype(BF)
        ds_own[i] = ds[0:TOK]
        dq_ref[:, lanes] = (dot(ds, kb[:, lanes], TN) * scale).astype(BF)
        return carry

    lax.fori_loop(0, HEADS, own_head, 0, unroll=UNROLL)
    over_quarters(1)

    def key_head(i, carry):
        h = 8 * lax.rem(i, 2) + lax.div(i, 2)
        lanes = head_lanes(h)
        later = dab[i, TOK:, :]
        p = probs_k[i]
        dprobs = dot(vb[own, lanes], later, NT)
        ds = (p * (dprobs - jnp.concatenate([delta[1, i], delta[2, i]], axis=1))).astype(BF)
        dkey = dot(ds_own[i], qb[own, lanes], NN) + dot(ds, qb[TOK:, lanes], NN)
        dk_ref[:, lanes] = (dkey * scale).astype(BF)
        dval = dot(probs[i, 0:TOK, :].astype(BF), dab[i, 0:TOK, :], NN) + dot(p.astype(BF), later, NN)
        dv_ref[:, lanes] = dval.astype(BF)
        return carry


    def d_wo_sum():
        quarter_in[zq, zt] = jnp.zeros((32, 256), BF)
        took(zin.at[pl.ds(0, 3), 0, 0], rq_r)
        total = near_sum[zq, zt]
        for i in range(4):
            total = total + quarter_in[i // 2, i % 2].astype(F32)
        grad_scale = 1.0 / math.sqrt(8 * n_ctx * TOK)
        mine_f[...] = total * grad_scale
        for d in x_group:
            send(mine_f, fin.at[core * NX + x], rf_s, rf_r, x_peer(*d)[0])
        fin[core * NX + x] = mine_f[...]

    def from_next(slot):
        took(chunk(slot, far), fw_r.at[slot])
        took(deltas(slot, 2), ds_r.at[slot])

        @pl.when(core == 0)
        def _():
            send(chunk(slot, far), chunk(slot, near), fo_s.at[slot], fo_r.at[slot], other)
            send(deltas(slot, 2), deltas(slot, 1), dn_s.at[slot], dn_r.at[slot], other)

    def from_other(slot):
        took(chunk(slot, near), fo_r.at[slot])
        took(deltas(slot, 1), dn_r.at[slot])
        key_head(2 * slot, 0)
        key_head(2 * slot + 1, 0)

    def key_step(j, carry):
        from_next(turn(j))
        from_other(turn(j - 1))
        return carry

    from_next(turn(0))
    lax.fori_loop(1, 6, key_step, 0)
    d_wo_sum()
    lax.fori_loop(6, SLOTS, key_step, 0)
    from_other(turn(SLOTS - 1))

    took(fin.at[pl.ds(0, 7)], rf_r)
    turned[...] = fin[...].reshape(2 * DH, 256).T
    dw_ref[...] = turned[pl.ds(pl.multiple_of((2 * x + core) * 32, 32), 32), :]

    took(wt_in.at[:, pl.ds(0, DH)], wc_s)
    for dz in Z_OFFSETS:
        took(w_piece(x, z), wz_s.at[dz])
    took(wt.at[:, :, pl.ds(0, 3)], wx_s)
    for part in range(2):
        for dx in (1, 3, 2):
            took(xin.at[part, dx], rx_s.at[part, dx])
    for part in range(2):
        for i in range(2):
            took(zin.at[i, part], rz_s.at[part, i])
            took(zin.at[2, part, i], rz_s.at[part, 2 + i])
        for top in range(2):
            @pl.when((zq != part) | (zt != top))
            def _():
                took(quarter_out.at[part, top], rq_s.at[part, top])
    took(fin.at[pl.ds(0, 7)], rf_s)
    for i in range(6):
        took(half(me, 0), g_s.at[i])
    for i in range(6, 10):
        took(whole(me), g_s.at[i])
    took(sb.at[pl.ds(0, 896), :], sa_s)
    for i in range(4):
        took(kb.at[own, :], kv_s.at[i])
    for i in range(2):
        took(lse.at[0], row_s.at[i])
    for i in range(2):
        took(qb.at[own, :], q_s.at[i])
    for slot in range(SLOTS):
        @pl.when(slot != me)
        def _():
            took(dsend.at[0], da_s.at[slot])

    for slot in range(SLOTS):
        took(chunk(slot, own), fw_s.at[slot])
        took(chunk(slot, own), fo_s.at[slot])
        took(deltas(slot, 0), ds_s.at[slot])
        took(deltas(slot, 0), dn_s.at[slot])


def per_device(queries, keys, values, saved_output, d_out, w_out, block_order):
    sems = pltpu.SemaphoreType.DMA
    vmem = pltpu.VMEM
    tokens = jax.ShapeDtypeStruct((TOK, FEAT), BF)
    anywhere = pl.BlockSpec(memory_space=pltpu.HBM)
    inside = pl.BlockSpec(memory_space=pltpu.VMEM)
    dq, dk, dv, dw = pl.pallas_call(
        kernel,
        out_shape=(tokens, tokens, tokens, jax.ShapeDtypeStruct((32, 256), F32)),
        in_specs=[pl.BlockSpec(memory_space=pltpu.SMEM)] + [anywhere] * 5 + [inside],
        out_specs=(inside,) * 4,
        scratch_shapes=[
            vmem((3 * TOK, FEAT), BF),
            vmem((3 * TOK, FEAT), BF),
            vmem((3 * TOK, FEAT), BF),
            vmem((TOK, FEAT), BF),
            vmem((SLOTS * TOK, FEAT), BF),
            vmem((HEADS, 3 * TOK, DH), BF),
            vmem((3, HEADS, 1, TOK), F32),
            vmem((3, HEADS, 1, TOK), F32),
            vmem((2, NZL, NX, 64, DH), BF),
            vmem((FEAT, 2 * DH), BF),
            vmem((SLOTS * TOK, 2 * DH), BF),
            vmem((2 * DH, SLOTS * TOK), BF),
            vmem((SLOTS, 2, TOK, DH), BF),
            vmem((HEADS, 3 * TOK, TOK), F32),
            vmem((HEADS, TOK, 2 * TOK), F32),
            vmem((HEADS, TOK, TOK), BF),
            vmem((5, TOK, TOK), F32),
            vmem((2, NX, 32, FEAT), F32),
            vmem((2, NX, 32, FEAT), BF),
            vmem((2, NX, 2, 32, 1024), BF),
            vmem((4, 2, 2, 32, 256), F32),
            vmem((4, 2, 2, 32, 256), BF),
            vmem((3, 2, 2, 32, 256), BF),
            vmem((2, 2, 32, 256), F32),
            vmem((2, 2, 32, 256), BF),
            vmem((2, 2, 32, 256), BF),
            vmem((32, 256), F32),
            vmem((2 * NX, 32, 256), F32),
            vmem((256, 2 * DH), F32),
            sems((5,)),
            sems,
            sems,
            sems((NZ,)),
            sems((NZ,)),
            sems,
            sems,
            sems((10,)),
            sems((10,)),
            sems,
            sems,
            sems((4,)),
            sems((4,)),
            sems((2,)),
            sems((2,)),
            sems((8,)),
            sems((8,)),
            sems((8,)),
            sems((8,)),
            sems((8,)),
            sems((8,)),
            sems((2,)),
            sems((2,)),
            sems((8,)),
            sems((8,)),
            sems((8,)),
            sems((8,)),
            sems((2, NX)),
            sems((2, NX)),
            sems((2, 4)),
            sems((2, 4)),
            sems((2, 2)),
            sems,
            sems,
            sems,
        ],
        compiler_params=pltpu.CompilerParams(
            collective_id=0, has_side_effects=True, vmem_limit_bytes=60 * 1024 * 1024
        ),
    )(block_order, queries[0], keys[0], values[0], saved_output[0], d_out[0], w_out.T)
    return dq[None], dk[None], dv[None], dw.T


def solution(mesh):
    tokens = P("dp", "ctx", None)
    return jax.shard_map(
        per_device,
        mesh=mesh,
        in_specs=(tokens,) * 5 + (P("dp", "ctx"), P()),
        out_specs=(tokens,) * 3 + (P("dp", "ctx"),),
        check_vma=False,
    )
```

```python
import math

import jax
import jax.numpy as jnp
from jax import lax
from jax.experimental import pallas as pl
from jax.experimental.pallas import tpu as pltpu
from jax.sharding import PartitionSpec as P

DH = 128
TOK = 128
HEADS = 16
FEAT = 2048
NX, NY, NZ, NZL = 4, 4, 16, 8
SLOTS = 2 * NY
Z_OFFSETS = (1, 15, 2, 14, 3, 13, 4, 12, 5, 11, 6, 10, 7, 9, 8)
MESH = pl.DeviceIdType.MESH
UNROLL = 8
BF = jnp.bfloat16
F32 = jnp.float32

NT = (((1,), (1,)), ((), ()))
NN = (((1,), (0,)), ((), ()))
TN = (((0,), (0,)), ((), ()))


def dot(a, b, dims):
    return lax.dot_general(a, b, dims, preferred_element_type=F32)


def kernel(
    order_ref, q_in, k_in, v_in, saved_in, grad_in, wt_in,
    dq_ref, dk_ref, dv_ref, dw_ref,
    qb, kb, vb, sv, gb, dab, lse, delta,
    wt, ww, sb, st, dsend, probs, probs_k, ds_own, bias,
    dwp, dwb, xin, xsum, zout, zin, near_sum, quarter_out, quarter_in, mine_f, fin, turned,
    load_s, wc_s, wc_r, wz_s, wz_r, wx_s, wx_r, g_s, g_r, sa_s, sa_r, kv_s, kv_r, q_s, q_r,
    da_s, da_r, fw_s, fw_r, fo_s, fo_r, row_s, row_r, ds_s, ds_r, dn_s, dn_r, rx_s, rx_r, rz_s, rz_r, rq_s, rq_r, rf_s, rf_r,
):
    ctx = lax.axis_index("ctx")
    dp = lax.axis_index("dp")
    core = lax.rem(ctx, 2)
    x = lax.rem(lax.div(ctx, 2), NX)
    zl = lax.div(ctx, 2 * NX)
    y = lax.rem(dp, NY)
    z = lax.div(dp, NY) * NZL + zl
    n_ctx = 2 * NX * NZL
    me = 2 * y + core
    zt, zq, zr = lax.div(z, NZL), lax.div(zl, 4), lax.rem(zl, 4)

    def at(xx, yy, zz, cc):
        return {
            "ctx": lax.rem(zz, NZL) * (2 * NX) + xx * 2 + cc,
            "dp": lax.div(zz, NZL) * NY + yy,
        }

    other = at(x, y, z, 1 - core)
    after = {"ctx": lax.rem(ctx + 2, n_ctx), "dp": dp}
    before = {"ctx": lax.rem(ctx + n_ctx - 2, n_ctx), "dp": dp}
    yp, ym, yf = lax.rem(y + 1, NY), lax.rem(y + 3, NY), lax.rem(y + 2, NY)
    y_up, y_down = at(x, yp, z, core), at(x, ym, z, core)
    y_group = [(dy, dc) for dy in (1, 3, 2, 0) for dc in (0, 1) if (dy, dc) != (0, 0)]
    x_group = [(dx, dc) for dx in (1, 3, 2, 0) for dc in (0, 1) if (dx, dc) != (0, 0)]

    def y_peer(dy, dc):
        yy, cc = lax.rem(y + dy, NY), lax.rem(core + dc, 2)
        return at(x, yy, z, cc), 2 * yy + cc

    def x_peer(dx, dc):
        xx, cc = lax.rem(x + dx, NX), lax.rem(core + dc, 2)
        return at(xx, y, z, cc), xx, cc

    def send(src, dst, ssem, rsem, device):
        copy = pltpu.make_async_remote_copy(
            src_ref=src, dst_ref=dst, send_sem=ssem, recv_sem=rsem, device_id=device, device_id_type=MESH
        )
        copy.start()

    def took(ref, sem):
        pltpu.make_async_copy(ref, ref, sem).wait()

    own = pl.ds(0, TOK)
    my_rows = pl.ds(pl.multiple_of(me * TOK, TOK), TOK)
    loads = [
        pltpu.make_async_copy(grad_in, gb.at[my_rows, :], load_s.at[0]),
        pltpu.make_async_copy(saved_in, sv, load_s.at[1]),
        pltpu.make_async_copy(k_in, kb.at[own, :], load_s.at[2]),
        pltpu.make_async_copy(q_in, qb.at[own, :], load_s.at[3]),
        pltpu.make_async_copy(v_in, vb.at[own, :], load_s.at[4]),
    ]
    for load in loads:
        load.start()

    barrier = pltpu.get_barrier_semaphore()
    peers = [y_peer(*d)[0] for d in y_group] + [x_peer(*d)[0] for d in x_group if d != (0, 1)]
    peers += [at(x, y, lax.rem(z + dz, NZ), core) for dz in Z_OFFSETS] + [after, before]
    for peer in peers:
        pl.semaphore_signal(barrier, inc=1, device_id=peer, device_id_type=MESH)
    pl.semaphore_wait(barrier, len(peers))

    def w_piece(xx, zz):
        return wt.at[lax.div(zz, NZL), lax.rem(zz, NZL), xx]

    def half_lanes(cc):
        return pl.ds(pl.multiple_of(cc * DH, DH), DH)

    zh = lax.div(z, NZL)
    piece = pl.ds(pl.multiple_of(core * 32, 32), 32)
    send(wt_in.at[:, half_lanes(1 - core)], wt.at[zh, zl, x, piece], wc_s, wc_r, other)
    wt[zh, zl, x, piece] = wt_in[:, half_lanes(core)]
    def half(slot, part):
        return gb.at[pl.ds(pl.multiple_of(slot * TOK + part * 64, 64), 64), :]

    def whole(slot):
        return gb.at[pl.ds(pl.multiple_of(slot * TOK, TOK), TOK), :]

    s_up, s_down, s_far = 2 * yp + core, 2 * ym + core, 2 * yf + core
    loads[0].wait()
    send(half(me, 0), half(me, 0), g_s.at[0], g_r.at[0], y_up)
    send(half(me, 1), half(me, 1), g_s.at[1], g_r.at[1], y_down)
    send(half(me, 1), half(me, 1), g_s.at[2], g_r.at[2], y_up)
    send(half(me, 0), half(me, 0), g_s.at[3], g_r.at[3], y_down)
    send(whole(me), whole(me), g_s.at[6], g_r.at[6], other)
    took(wt_in.at[:, pl.ds(0, DH)], wc_r)
    for dz in Z_OFFSETS:
        send(w_piece(x, z), w_piece(x, z), wz_s.at[dz], wz_r.at[dz], at(x, y, lax.rem(z + dz, NZ), core))

    prev2, prev1 = pl.ds(2 * TOK, TOK), pl.ds(TOK, TOK)
    loads[2].wait()
    loads[3].wait()

    def head_lanes(h):
        return pl.ds(pl.multiple_of(h * DH, DH), DH)


    def keys_and_queries(first, rows):
        def part(start):
            return pl.ds(start + first, rows)

        @pl.when(x != NX - 1)
        def _():
            send(kb.at[part(0), :], kb.at[part(2 * TOK), :], kv_s.at[0], kv_r.at[0], after)

        @pl.when(x != 0)
        def _():
            send(qb.at[part(0), :], qb.at[part(2 * TOK), :], q_s.at[0], q_r.at[0], before)

    keys_and_queries(0, 32)

    @pl.when(x == NX - 1)
    def _():
        send(kb.at[own, :], kb.at[prev2, :], kv_s.at[0], kv_r.at[0], after)

    @pl.when(x == 0)
    def _():
        send(qb.at[own, :], qb.at[prev2, :], q_s.at[0], q_r.at[0], before)

    loads[4].wait()
    loads[1].wait()
    for zh in range(2):
        sb[my_rows, pl.ds(zh * DH, DH)] = sv[:, head_lanes(8 * zh + me)]

    group = ctx
    lane = lax.broadcasted_iota(jnp.int32, (TOK, TOK), 1)
    row = lax.broadcasted_iota(jnp.int32, (TOK, TOK), 0)

    def places(g, index):
        first, second = order_ref[2 * g], order_ref[2 * g + 1]
        return jnp.where(index < 64, first * 64 + index, second * 64 + index - 64)

    def blocked(key_group, query_group):
        seen = places(key_group, row) <= places(query_group, lane)
        return jnp.where(seen, 0.0, -1e30).astype(F32)

    def shifted(by):
        return lax.rem(group + n_ctx + by, n_ctx)

    bias[0] = blocked(group, group)
    bias[1] = blocked(shifted(-1), group)
    bias[2] = blocked(shifted(-2), group)
    bias[3] = blocked(group, shifted(1))
    bias[4] = blocked(group, shifted(2))
    scale = 1.0 / math.sqrt(DH)

    def own_scores(i, carry):
        lanes = head_lanes(8 * lax.rem(i, 2) + lax.div(i, 2))
        probs[i, 0:TOK] = dot(kb[own, lanes], qb[own, lanes], NT) * scale + bias[0]
        return carry

    lax.fori_loop(0, HEADS, own_scores, 0, unroll=UNROLL)

    def z_peer(dz):
        return at(x, y, lax.rem(z + dz, NZ), core)

    def rest_of(d):
        return lax.rem(zr + d, 4)

    def w_across(zz):
        for i, dx in enumerate((1, 3, 2)):
            send(w_piece(x, zz), w_piece(x, zz), wx_s, wx_r, at(lax.rem(x + dx, NX), y, z, core))

    w_across(z)
    for i, dz in enumerate(Z_OFFSETS):
        zz = lax.rem(z + dz, NZ)
        took(w_piece(x, zz), wz_r.at[NZ - dz])
        w_across(zz)
        if i == 5:
            took(half(s_down, 0), g_r.at[0])
            send(half(s_down, 0), half(s_down, 0), g_s.at[4], g_r.at[4], y_up)
            took(half(s_up, 1), g_r.at[1])
            send(half(s_up, 1), half(s_up, 1), g_s.at[5], g_r.at[5], y_down)
            for d in y_group:
                dev, slot = y_peer(*d)
                for top in range(2):
                    send(sv.at[:, head_lanes(8 * top + slot)], sb.at[my_rows, pl.ds(top * DH, DH)], sa_s, sa_r, dev)
    keys_and_queries(32, 96)

    @pl.when(core == 0)
    def _():
        send(kb.at[own, :], kb.at[prev1, :], kv_s.at[2], kv_r.at[2], other)
        send(vb.at[own, :], vb.at[prev1, :], kv_s.at[3], kv_r.at[3], other)

    @pl.when(core == 1)
    def _():
        send(qb.at[own, :], qb.at[prev1, :], q_s.at[1], q_r.at[1], other)

    took(half(s_down, 1), g_r.at[2])
    send(whole(s_down), whole(s_down), g_s.at[7], g_r.at[7], other)
    took(half(s_up, 0), g_r.at[3])
    send(whole(s_up), whole(s_up), g_s.at[8], g_r.at[8], other)
    took(wt.at[:, :, pl.ds(0, 3)], wx_r)
    send(vb.at[own, :], vb.at[prev2, :], kv_s.at[1], kv_r.at[1], after)

    took(half(s_far, 0), g_r.at[4])
    took(half(s_far, 1), g_r.at[5])
    send(whole(s_far), whole(s_far), g_s.at[9], g_r.at[9], other)
    for i in range(6, 10):
        took(whole(me), g_r.at[i])

    ww[:, 0:DH] = wt[0].reshape(FEAT, DH)
    ww[:, DH:] = wt[1].reshape(FEAT, DH)
    def attn_step(j, carry):
        dy = 2 - j + 3 * lax.div(j, 2) - 2 * lax.div(j, 3)
        yy = lax.rem(y + dy, NY)
        rows = pl.ds(pl.multiple_of(yy * 256, 256), 256)
        part = dot(gb[rows, :], ww[...], NN).astype(BF)
        for cc in range(2):
            slot = 2 * yy + cc
            for top in range(2):
                dsend[slot, top] = part[cc * TOK : (cc + 1) * TOK, top * DH : (top + 1) * DH]

            @pl.when(slot != me)
            def _():
                send(
                    dsend.at[slot], dab.at[pl.ds(2 * me, 2), own, :], da_s.at[slot], da_r.at[me],
                    at(x, yy, z, cc),
                )
        return carry

    lax.fori_loop(0, 4, attn_step, 0, unroll=2)
    for top in range(2):
        dab[2 * me + top, 0:TOK, :] = dsend[me, top]

    took(sb.at[pl.ds(0, 896), :], sa_r)
    st[...] = sb[...].astype(F32).T.astype(BF)

    def part_lanes(part):
        return pl.ds(part * 1024, 1024)

    def partial_sums(low, carry):
        lanes = pl.ds(pl.multiple_of(low * 256, 256), 256)
        sums = dot(st[...], gb[:, lanes], NN).reshape(2, NX, 32, 256)
        dwp[:, :, :, lanes] = sums
        dwb[:, :, :, lanes] = sums.astype(BF)
        return carry

    for part in range(2):
        lax.fori_loop(4 * part, 4 * part + 4, partial_sums, 0)
        for dx in (1, 3, 2):
            xx = lax.rem(x + dx, NX)
            send(
                dwb.at[:, xx, :, part_lanes(part)], xin.at[part, dx], rx_s.at[part, dx], rx_r.at[part, dx],
                at(xx, y, z, core),
            )


    def over_z(part):
        sums = dwp[:, x, :, part_lanes(part)]
        for dx in (1, 3, 2):
            took(xin.at[part, dx], rx_r.at[part, dx])
            sums = sums + xin[part, dx].astype(F32)
        for top in range(2):
            for rest in range(4):
                block = sums[top, :, rest * 256 : (rest + 1) * 256]
                xsum[rest, part, top] = block
                zout[rest, part, top] = block.astype(BF)
        send(zout.at[rest_of(1), part], zin.at[0, part], rz_s.at[part, 0], rz_r.at[part, 0], z_peer(1))
        send(zout.at[rest_of(3), part], zin.at[1, part], rz_s.at[part, 1], rz_r.at[part, 1], z_peer(15))
        send(zout.at[rest_of(2), part, 0], zin.at[2, part, 0], rz_s.at[part, 2], rz_r.at[part, 2], z_peer(2))
        send(zout.at[rest_of(2), part, 1], zin.at[2, part, 1], rz_s.at[part, 3], rz_r.at[part, 3], z_peer(14))

    def over_quarters(part):
        for i in range(2):
            took(zin.at[i, part], rz_r.at[part, i])
            took(zin.at[2, part, i], rz_r.at[part, 2 + i])
        sums = xsum[zr, part]
        for i in range(3):
            sums = sums + zin[i, part].astype(F32)
        near_sum[part] = sums
        quarter_out[part] = sums.astype(BF)
        for top in range(2):
            @pl.when((zq != part) | (zt != top))
            def _():
                send(
                    quarter_out.at[part, top], quarter_in.at[zq, zt], rq_s.at[part, top], rq_r,
                    at(x, y, top * NZL + part * 4 + zr, core),
                )

    took(kb.at[prev2, :], kv_r.at[0])
    took(qb.at[prev2, :], q_r.at[0])

    @pl.when(core == 1)
    def _():
        send(kb.at[prev2, :], kb.at[prev1, :], kv_s.at[2], kv_r.at[2], other)

    @pl.when(core == 0)
    def _():
        send(qb.at[prev2, :], qb.at[prev1, :], q_s.at[1], q_r.at[1], other)

    took(kb.at[prev1, :], kv_r.at[2])

    def score_head(i, carry):
        h = 8 * lax.rem(i, 2) + lax.div(i, 2)
        lanes = head_lanes(h)
        s = dot(kb[TOK:, lanes], qb[own, lanes], NT) * scale + bias[1:3].reshape(2 * TOK, TOK)
        s = jnp.concatenate([probs[i, 0:TOK], s], axis=0)
        top = jnp.max(s, axis=0, keepdims=True)
        e = jnp.exp(s - top)
        total = jnp.sum(e, axis=0, keepdims=True)
        probs[i] = e * (1.0 / total)
        lse[0, i] = top + jnp.log(total)
        return carry

    lax.fori_loop(0, HEADS, score_head, 0, unroll=UNROLL)

    near, far = pl.ds(TOK, TOK), pl.ds(2 * TOK, TOK)
    send(lse.at[0], lse.at[2], row_s.at[0], row_r.at[0], before)

    @pl.when(core == 1)
    def _():
        send(lse.at[0], lse.at[1], row_s.at[1], row_r.at[1], other)

    def chunk(slot, rows):
        return dab.at[pl.ds(2 * slot, 2), rows, :]

    ones = jnp.ones((8, DH), BF)

    def deltas(slot, which):
        return delta.at[which, pl.ds(2 * slot, 2)]

    def pass_on(slot):
        @pl.when(slot != me)
        def _():
            took(chunk(slot, own), da_r.at[slot])

        send(chunk(slot, own), chunk(slot, far), fw_s.at[slot], fw_r.at[slot], before)

        @pl.when(core == 1)
        def _():
            send(chunk(slot, own), chunk(slot, near), fo_s.at[slot], fo_r.at[slot], other)

        for zh in range(2):
            i = 2 * slot + zh
            prod = dab[i, 0:TOK, :].astype(F32) * sv[:, head_lanes(8 * zh + slot)].astype(F32)
            high = prod.astype(BF)
            low = (prod - high.astype(F32)).astype(BF)
            sums = dot(ones, high, NT) + dot(ones, low, NT)
            delta[0, i] = sums[0:1]
        send(deltas(slot, 0), deltas(slot, 2), ds_s.at[slot], ds_r.at[slot], before)

        @pl.when(core == 1)
        def _():
            send(deltas(slot, 0), deltas(slot, 1), dn_s.at[slot], dn_r.at[slot], other)

    def turn(j):
        dy = lax.div(j, 2)
        dy = dy + lax.div(dy, 2) - 2 * lax.div(dy, 3)
        return 2 * lax.rem(y + dy, NY) + lax.rem(j, 2)

    def pass_step(j, carry):
        pass_on(turn(j))
        return carry

    lax.fori_loop(0, SLOTS, pass_step, 0)

    over_z(0)

    took(qb.at[near, :], q_r.at[1])
    took(lse.at[2], row_r.at[0])

    @pl.when(core == 0)
    def _():
        send(lse.at[2], lse.at[1], row_s.at[1], row_r.at[1], other)

    took(lse.at[1], row_r.at[1])

    def later_head(i, carry):
        h = 8 * lax.rem(i, 2) + lax.div(i, 2)
        lanes = head_lanes(h)
        s = dot(kb[own, lanes], qb[TOK:, lanes], NT) * scale
        s = s + jnp.concatenate([bias[3], bias[4]], axis=1)
        probs_k[i] = jnp.exp(s - jnp.concatenate([lse[1, i], lse[2, i]], axis=1))
        return carry

    lax.fori_loop(0, HEADS, later_head, 0, unroll=UNROLL)
    over_z(1)
    over_quarters(0)

    took(vb.at[prev2, :], kv_r.at[1])

    @pl.when(core == 1)
    def _():
        send(vb.at[prev2, :], vb.at[prev1, :], kv_s.at[3], kv_r.at[3], other)

    took(vb.at[prev1, :], kv_r.at[3])

    def own_head(i, carry):
        h = 8 * lax.rem(i, 2) + lax.div(i, 2)
        lanes = head_lanes(h)
        dprobs = dot(vb[:, lanes], dab[i, 0:TOK, :], NT)
        ds = (probs[i] * (dprobs - delta[0, i])).astype(BF)
        ds_own[i] = ds[0:TOK]
        dq_ref[:, lanes] = (dot(ds, kb[:, lanes], TN) * scale).astype(BF)
        return carry

    lax.fori_loop(0, HEADS, own_head, 0, unroll=UNROLL)
    over_quarters(1)

    def key_head(i, carry):
        h = 8 * lax.rem(i, 2) + lax.div(i, 2)
        lanes = head_lanes(h)
        later = dab[i, TOK:, :]
        p = probs_k[i]
        dprobs = dot(vb[own, lanes], later, NT)
        ds = (p * (dprobs - jnp.concatenate([delta[1, i], delta[2, i]], axis=1))).astype(BF)
        dkey = dot(ds_own[i], qb[own, lanes], NN) + dot(ds, qb[TOK:, lanes], NN)
        dk_ref[:, lanes] = (dkey * scale).astype(BF)
        dval = dot(probs[i, 0:TOK, :].astype(BF), dab[i, 0:TOK, :], NN) + dot(p.astype(BF), later, NN)
        dv_ref[:, lanes] = dval.astype(BF)
        return carry


    def d_wo_sum():
        quarter_in[zq, zt] = jnp.zeros((32, 256), BF)
        took(zin.at[pl.ds(0, 3), 0, 0], rq_r)
        total = near_sum[zq, zt]
        for i in range(4):
            total = total + quarter_in[i // 2, i % 2].astype(F32)
        grad_scale = 1.0 / math.sqrt(8 * n_ctx * TOK)
        mine_f[...] = total * grad_scale
        for d in x_group:
            send(mine_f, fin.at[core * NX + x], rf_s, rf_r, x_peer(*d)[0])
        fin[core * NX + x] = mine_f[...]

    def from_next(slot):
        took(chunk(slot, far), fw_r.at[slot])
        took(deltas(slot, 2), ds_r.at[slot])

        @pl.when(core == 0)
        def _():
            send(chunk(slot, far), chunk(slot, near), fo_s.at[slot], fo_r.at[slot], other)
            send(deltas(slot, 2), deltas(slot, 1), dn_s.at[slot], dn_r.at[slot], other)

    def from_other(slot):
        took(chunk(slot, near), fo_r.at[slot])
        took(deltas(slot, 1), dn_r.at[slot])
        key_head(2 * slot, 0)
        key_head(2 * slot + 1, 0)

    def key_step(j, carry):
        from_next(turn(j))
        from_other(turn(j - 1))
        return carry

    from_next(turn(0))
    lax.fori_loop(1, 6, key_step, 0)
    d_wo_sum()
    lax.fori_loop(6, SLOTS, key_step, 0)
    from_other(turn(SLOTS - 1))

    took(fin.at[pl.ds(0, 7)], rf_r)
    turned[...] = fin[...].reshape(2 * DH, 256).T
    dw_ref[...] = turned[pl.ds(pl.multiple_of((2 * x + core) * 32, 32), 32), :]

    took(wt_in.at[:, pl.ds(0, DH)], wc_s)
    for dz in Z_OFFSETS:
        took(w_piece(x, z), wz_s.at[dz])
    took(wt.at[:, :, pl.ds(0, 3)], wx_s)
    for part in range(2):
        for dx in (1, 3, 2):
            took(xin.at[part, dx], rx_s.at[part, dx])
    for part in range(2):
        for i in range(2):
            took(zin.at[i, part], rz_s.at[part, i])
            took(zin.at[2, part, i], rz_s.at[part, 2 + i])
        for top in range(2):
            @pl.when((zq != part) | (zt != top))
            def _():
                took(quarter_out.at[part, top], rq_s.at[part, top])
    took(fin.at[pl.ds(0, 7)], rf_s)
    for i in range(6):
        took(half(me, 0), g_s.at[i])
    for i in range(6, 10):
        took(whole(me), g_s.at[i])
    took(sb.at[pl.ds(0, 896), :], sa_s)
    for i in range(4):
        took(kb.at[own, :], kv_s.at[i])
    for i in range(2):
        took(lse.at[0], row_s.at[i])
    for i in range(2):
        took(qb.at[own, :], q_s.at[i])
    for slot in range(SLOTS):
        @pl.when(slot != me)
        def _():
            took(dsend.at[0], da_s.at[slot])

    for slot in range(SLOTS):
        took(chunk(slot, own), fw_s.at[slot])
        took(chunk(slot, own), fo_s.at[slot])
        took(deltas(slot, 0), ds_s.at[slot])
        took(deltas(slot, 0), dn_s.at[slot])


def per_device(queries, keys, values, saved_output, d_out, w_out, block_order):
    sems = pltpu.SemaphoreType.DMA
    vmem = pltpu.VMEM
    tokens = jax.ShapeDtypeStruct((TOK, FEAT), BF)
    anywhere = pl.BlockSpec(memory_space=pltpu.HBM)
    inside = pl.BlockSpec(memory_space=pltpu.VMEM)
    dq, dk, dv, dw = pl.pallas_call(
        kernel,
        out_shape=(tokens, tokens, tokens, jax.ShapeDtypeStruct((32, 256), F32)),
        in_specs=[pl.BlockSpec(memory_space=pltpu.SMEM)] + [anywhere] * 5 + [inside],
        out_specs=(inside,) * 4,
        scratch_shapes=[
            vmem((3 * TOK, FEAT), BF),
            vmem((3 * TOK, FEAT), BF),
            vmem((3 * TOK, FEAT), BF),
            vmem((TOK, FEAT), BF),
            vmem((SLOTS * TOK, FEAT), BF),
            vmem((HEADS, 3 * TOK, DH), BF),
            vmem((3, HEADS, 1, TOK), F32),
            vmem((3, HEADS, 1, TOK), F32),
            vmem((2, NZL, NX, 64, DH), BF),
            vmem((FEAT, 2 * DH), BF),
            vmem((SLOTS * TOK, 2 * DH), BF),
            vmem((2 * DH, SLOTS * TOK), BF),
            vmem((SLOTS, 2, TOK, DH), BF),
            vmem((HEADS, 3 * TOK, TOK), F32),
            vmem((HEADS, TOK, 2 * TOK), F32),
            vmem((HEADS, TOK, TOK), BF),
            vmem((5, TOK, TOK), F32),
            vmem((2, NX, 32, FEAT), F32),
            vmem((2, NX, 32, FEAT), BF),
            vmem((2, NX, 2, 32, 1024), BF),
            vmem((4, 2, 2, 32, 256), F32),
            vmem((4, 2, 2, 32, 256), BF),
            vmem((3, 2, 2, 32, 256), BF),
            vmem((2, 2, 32, 256), F32),
            vmem((2, 2, 32, 256), BF),
            vmem((2, 2, 32, 256), BF),
            vmem((32, 256), F32),
            vmem((2 * NX, 32, 256), F32),
            vmem((256, 2 * DH), F32),
            sems((5,)),
            sems,
            sems,
            sems((NZ,)),
            sems((NZ,)),
            sems,
            sems,
            sems((10,)),
            sems((10,)),
            sems,
            sems,
            sems((4,)),
            sems((4,)),
            sems((2,)),
            sems((2,)),
            sems((8,)),
            sems((8,)),
            sems((8,)),
            sems((8,)),
            sems((8,)),
            sems((8,)),
            sems((2,)),
            sems((2,)),
            sems((8,)),
            sems((8,)),
            sems((8,)),
            sems((8,)),
            sems((2, NX)),
            sems((2, NX)),
            sems((2, 4)),
            sems((2, 4)),
            sems((2, 2)),
            sems,
            sems,
            sems,
        ],
        compiler_params=pltpu.CompilerParams(
            collective_id=0, has_side_effects=True, vmem_limit_bytes=60 * 1024 * 1024
        ),
    )(block_order, queries[0], keys[0], values[0], saved_output[0], d_out[0], w_out.T)
    return dq[None], dk[None], dv[None], dw.T


def solution(mesh):
    tokens = P("dp", "ctx", None)
    return jax.shard_map(
        per_device,
        mesh=mesh,
        in_specs=(tokens,) * 5 + (P("dp", "ctx"), P()),
        out_specs=(tokens,) * 3 + (P("dp", "ctx"),),
        check_vma=False,
    )
```
